256 devices in a mesh: src: 8 (over y, core), tgt: 32 (over x, z).
Axes of the slice: x: 4, y: 4, z: 8, core: 2. Of those that a mesh axis runs over, the one named last changes fastest.
Arguments:
- source: bfloat16 [16384, 128], P('src'), may hold values from -6 to 6
- target: bfloat16 [32768, 128], P('tgt'), may hold values from -5 to 5
- start_map: float32 [128, 128], replicated, may hold values from -1 to 1
- warm_potential: float32 [32768], P('tgt'), may hold values from -60 to 24
Outputs:
- row_potential: float32 [16384], P('src')
- col_potential: float32 [32768], P('tgt')
- new_map: float32 [128, 128], replicated
The draws below stay inside these ranges and needn't reach their ends.
All inputs are finite; a program needn't handle non-finite values.
Results may differ from the reference program's by a relative error of at most 0.0078.
Values sent between devices are 32-bit elements; how exact they have to be, the bound alone decides.
A program may use at most 64 MiB of HBM per device.

```python
import math
import jax
import jax.numpy as jnp
from jax import lax

D = 128
ROUNDS = 3
NEWTON = 10
NS = 16384
NT = 32768


def butterfly(key):
    matrix = jnp.eye(D, dtype=jnp.float32)
    stride = 1
    section_index = 0
    while stride < D:
        angles = jax.random.uniform(jax.random.fold_in(key, section_index), (D // (2 * stride), stride, 1), jnp.float32, -math.pi, math.pi)
        cosine = jnp.cos(angles)
        sine_vals = jnp.sin(angles)
        shaped = matrix.reshape(D // (2 * stride), 2, stride, D)
        upper_rows = shaped[:, 0]
        lower_rows = shaped[:, 1]
        new_upper = cosine * upper_rows - sine_vals * lower_rows
        new_lower = sine_vals * upper_rows + cosine * lower_rows
        matrix = jnp.stack([new_upper, new_lower], axis=1).reshape(D, D)
        stride = stride * 2
        section_index = section_index + 1
    row_order = jax.random.permutation(jax.random.fold_in(key, 99), D)
    return matrix[row_order]


def faint_rows(key):
    spacing = NT // 16
    offsets = jax.random.randint(jax.random.fold_in(key, 21), (16,), 2, spacing)
    return jnp.arange(16, dtype=jnp.int32) * spacing + offsets


def joint(key):
    rotation = butterfly(jax.random.fold_in(key, 11))
    source_key = jax.random.fold_in(key, 12)
    target_key = jax.random.fold_in(key, 13)
    source = jnp.clip(jax.random.normal(source_key, (NS, D), jnp.float32), -5.0, 5.0)
    target = jnp.clip(jax.random.normal(target_key, (NT, D), jnp.float32), -5.0, 5.0)
    faint = faint_rows(key)
    target = target.at[faint].multiply(0.02)
    return (source, target, rotation)


def draw_source(key, part):
    return joint(key)[0].astype(jnp.bfloat16)


def draw_target(key, part):
    return joint(key)[1].astype(jnp.bfloat16)


def draw_start_map(key, part):
    return joint(key)[2]


def draw_warm_potential(key, part):
    faint = faint_rows(key)
    key = jax.random.fold_in(key, 5)
    values = jnp.clip(4.0 * jax.random.normal(key, (NT,), jnp.float32), -24.0, 24.0)
    return values.at[faint].set(-60.0)


def setup_inputs(seed: int = 0) -> dict:
    key_list = jax.random.split(jax.random.key(seed), 5)
    return {
        "source": draw_source(jax.random.fold_in(key_list[4], 71), 0),
        "target": draw_target(jax.random.fold_in(key_list[4], 71), 0),
        "start_map": draw_start_map(jax.random.fold_in(key_list[4], 71), 0),
        "warm_potential": draw_warm_potential(jax.random.fold_in(key_list[4], 71), 0),
    }


EPS = 0.05

def row_lse_all(rotated, target, col_pot, score_scale):
    row_count = rotated.shape[0]
    block_rows = math.gcd(row_count, 512)
    blocks = rotated.reshape(row_count // block_rows, block_rows, rotated.shape[1])

    def one_block(row_block):
        scores = jnp.dot(row_block, target.T, preferred_element_type=jnp.float32) * score_scale + col_pot[None, :]
        return jax.nn.logsumexp(scores, axis=1)
    return lax.map(one_block, blocks).reshape(row_count)

def col_lse_all(rotated, target, row_pot, score_scale):
    row_count = rotated.shape[0]
    block_rows = math.gcd(row_count, 512)
    blocks = rotated.reshape(row_count // block_rows, block_rows, rotated.shape[1])
    pots = row_pot.reshape(row_count // block_rows, block_rows)

    def one_block(inputs):
        row_block, pot_block = inputs
        scores = jnp.dot(row_block, target.T, preferred_element_type=jnp.float32) * score_scale + pot_block[:, None]
        return jax.nn.logsumexp(scores, axis=0)
    return jax.nn.logsumexp(lax.map(one_block, (blocks, pots)), axis=0)

def covariance(source, rotated, target, col_pot, row_lse, score_scale):
    row_count = rotated.shape[0]
    block_rows = math.gcd(row_count, 512)
    nblocks = row_count // block_rows
    width = rotated.shape[1]

    def one_block(inputs):
        source_block, row_block, lse_block = inputs
        scores = jnp.dot(row_block, target.T, preferred_element_type=jnp.float32) * score_scale + col_pot[None, :] - lse_block[:, None]
        weights = jnp.exp(scores).astype(jnp.bfloat16)
        bary = jnp.dot(weights, target, preferred_element_type=jnp.float32)
        return jnp.dot(source_block.astype(jnp.float32).T, bary, precision=lax.Precision.HIGHEST)
    parts_sum = lax.map(one_block, (source.reshape(nblocks, block_rows, width), rotated.reshape(nblocks, block_rows, width), row_lse.reshape(nblocks, block_rows)))
    return lax.optimization_barrier(jnp.sum(parts_sum, axis=0))

def polar(matrix):
    iterate = matrix / jnp.sqrt(jnp.sum(matrix * matrix) + 1e-06)
    for newton_index in range(NEWTON):
        gram_matrix = jnp.dot(iterate.T, iterate, precision=lax.Precision.HIGHEST)
        iterate = 1.5 * iterate - 0.5 * jnp.dot(iterate, gram_matrix, precision=lax.Precision.HIGHEST)
    return iterate

def reference(source, target, start_map, warm_potential):
    score_scale = 1.0 / (math.sqrt(D) * EPS)
    rotated = jnp.dot(source, start_map.astype(jnp.bfloat16), preferred_element_type=jnp.float32).astype(jnp.bfloat16)
    col_pot = warm_potential
    for round_index in range(ROUNDS):
        row_pot = -math.log(NS) - row_lse_all(rotated, target, col_pot, score_scale)
        col_pot = -math.log(NT) - col_lse_all(rotated, target, row_pot, score_scale)
    row_lse = row_lse_all(rotated, target, col_pot, score_scale)
    row_pot = -math.log(NS) - row_lse
    new_map = polar(covariance(source, rotated, target, col_pot, row_lse, score_scale))
    return (EPS * row_pot, EPS * col_pot, new_map)
```

```python
import functools
import math

import jax
import jax.numpy as jnp
from jax import lax
from jax.experimental import pallas as pl
from jax.experimental.pallas import tpu as pltpu
from jax.sharding import PartitionSpec as P

ROUNDS = 3
NEWTON = 10
EPS = 0.05
LN2 = math.log(2.0)
MESH = pl.DeviceIdType.MESH
F32 = jnp.float32
BF16 = jnp.bfloat16
NX, NY, NZ, NC = 4, 4, 8, 2
NSRC = NY * NC
L = 128


def split(value):
    high = value.astype(BF16)
    low = (value - high.astype(F32)).astype(BF16)
    return high, low


def dot_nt(a, b):
    return lax.dot_general(a, b, (((1,), (1,)), ((), ())), preferred_element_type=F32)


def dot_nn(a, b):
    return jnp.dot(a, b, preferred_element_type=F32)


def lse2(parts):
    peak = parts[0]
    for part in parts[1:]:
        peak = jnp.maximum(peak, part)
    total = jnp.exp2(parts[0] - peak)
    for part in parts[1:]:
        total = total + jnp.exp2(part - peak)
    return peak + jnp.log2(total)


def total_of(parts):
    total = parts[0]
    for part in parts[1:]:
        total = total + part
    return total


def kernel(
    rows_all,
    cols_all,
    source_ref,
    target_ref,
    map_ref,
    warm_ref,
    row_out,
    col_out,
    map_out,
    rot,
    e_f32,
    e_b16,
    src_t,
    tgt_t,
    bary,
    u_t,
    cross,
    row_z,
    row_x,
    col_s,
    cross_s,
    cross_z,
    cross_x,
    cross_g,
    send_sem,
    recv_sem,
):
    rows, width = source_ref.shape
    cols = target_ref.shape[0]
    nb, nk = rows // L, cols // L
    scale2 = 1.0 / (math.sqrt(width) * EPS) / LN2
    me_s = lax.axis_index("src")
    me_t = lax.axis_index("tgt")
    me_x, me_z = me_t // NZ, lax.rem(me_t, NZ)
    peers_s = [(lax.rem(me_s + k, NSRC), me_t) for k in (4, 3, 5, 2, 6, 1, 7)]
    peers_z = [(me_s, me_x * NZ + lax.rem(me_z + k, NZ)) for k in (4, 3, 5, 2, 6, 1, 7)]
    peers_x = [(me_s, lax.rem(me_x + k, NX) * NZ + me_z) for k in (2, 1, 3)]

    barrier = pltpu.get_barrier_semaphore()
    everyone = peers_s + peers_z + peers_x
    for peer in everyone:
        pl.semaphore_signal(barrier, inc=1, device_id=peer, device_id_type=MESH)

    pending = []

    def send(phase, buf, me, peers):
        for peer in peers:
            pltpu.make_async_remote_copy(
                src_ref=buf.at[me],
                dst_ref=buf.at[me],
                send_sem=send_sem.at[phase],
                recv_sem=recv_sem.at[phase],
                device_id=peer,
                device_id_type=MESH,
            ).start()
        others = buf.at[pl.ds(0, len(peers))]
        done = pltpu.make_async_remote_copy(
            src_ref=others,
            dst_ref=others,
            send_sem=send_sem.at[phase],
            recv_sem=recv_sem.at[phase],
            device_id=peers[0],
            device_id_type=MESH,
        )
        pending.append(done)
        return done

    lane = lax.broadcasted_iota(jnp.int32, (L, L), 1)
    zero_tile = jnp.zeros((L, L), F32)

    def chunk(k):
        return pl.ds(k * L, L)

    rot[...] = dot_nn(source_ref[...], map_ref[...].astype(BF16)).astype(BF16)
    warm2 = warm_ref[...] * (1.0 / LN2)
    wide = 256
    for k in range(cols // wide):
        part = target_ref[pl.ds(k * wide, wide), :]
        warm_part = warm2[:, k * wide : (k + 1) * wide]

        def score_block(a, carry):
            block = rot[pl.ds(pl.multiple_of(a * 512, 512), 512), :]
            e_f32[pl.ds(a * 4, 4), :, pl.ds(k * wide, wide)] = (
                dot_nt(block, part) * scale2 + warm_part
            ).reshape(4, L, wide)
            return carry

        lax.fori_loop(0, rows // 512, score_block, 0)

    def first_row(a, acc):
        peak = e_f32[a, :, chunk(0)]
        for k in range(1, nk):
            peak = jnp.maximum(peak, e_f32[a, :, chunk(k)])
        peak = jnp.max(peak, axis=1, keepdims=True)
        total = jnp.exp2(e_f32[a, :, chunk(0)] - peak)
        for k in range(1, nk):
            total = total + jnp.exp2(e_f32[a, :, chunk(k)] - peak)
        total = jnp.sum(total, axis=1, keepdims=True)
        return jnp.where(lane == a, peak + jnp.log2(total), acc)

    first = lax.fori_loop(0, nb, first_row, zero_tile, unroll=2)
    pl.semaphore_wait(barrier, len(everyone))

    def row_reduce(index, tile, combine, meanwhile=None, meanwhile2=None):
        row_z[index, me_z] = tile.T[:nb]
        done = send(3 * index, row_z.at[index], me_z, peers_z)
        if meanwhile is not None:
            meanwhile()
        done.wait_recv()
        row_x[index, me_x] = combine([row_z[index, i] for i in range(NZ)])
        done = send(3 * index + 1, row_x.at[index], me_x, peers_x)
        if meanwhile2 is not None:
            meanwhile2()
        done.wait_recv()
        return combine([row_x[index, i] for i in range(NX)])

    def col_reduce(index, combine):
        done = send(3 * index + 2, col_s.at[index], me_s, peers_s)
        done.wait_recv()
        return combine([col_s[index, i] for i in range(NSRC)])

    def spread(value):
        u_t[...] = jnp.concatenate([value, jnp.zeros((L - nb, L), F32)], axis=0).T

    def column_of(a):
        return jnp.sum(jnp.where(lane == a, u_t[...], 0.0), axis=1, keepdims=True)

    def fold(tile, op):
        parts = [tile[8 * i : 8 * i + 8] for i in range(L // 8)]
        while len(parts) > 1:
            parts = [op(parts[i], parts[i + 1]) for i in range(0, len(parts), 2)]
        return parts[0]

    def transposes():
        def one_source(a, carry):
            block = source_ref[pl.ds(pl.multiple_of(a * L, L), L), :].astype(F32)
            src_t[a] = block.T
            return carry

        lax.fori_loop(0, nb, one_source, 0)

        def one_target(a, carry):
            block = target_ref[pl.ds(pl.multiple_of(a * L, L), L), :].astype(F32)
            tgt_t[a] = block.T
            return carry

        lax.fori_loop(0, nk, one_target, 0)

    row_lse = row_reduce(0, first, lse2, transposes)
    f_first = -math.log2(rows_all) - row_lse
    spread(f_first)

    def first_col_peak(a, accs):
        f_col = column_of(a)
        return tuple(
            jnp.maximum(accs[k], fold(e_f32[a, :, chunk(k)] + f_col, jnp.maximum))
            for k in range(nk)
        )

    peaks = lax.fori_loop(
        0, nb, first_col_peak, tuple(jnp.full((8, L), -jnp.inf, F32) for _ in range(nk))
    )
    peaks = [jnp.max(p, axis=0, keepdims=True) for p in peaks]

    def first_col_sum(a, accs):
        f_col = column_of(a)
        out = []
        for k in range(nk):
            e_val = jnp.exp2((e_f32[a, :, chunk(k)] + f_col) - peaks[k])
            e_f32[a, :, chunk(k)] = e_val
            e_b16[a, :, chunk(k)] = e_val.astype(BF16)
            out.append(accs[k] + fold(e_val, jnp.add))
        return tuple(out)

    zeros = tuple(jnp.zeros((8, L), F32) for _ in range(nk))
    sums = lax.fori_loop(0, nb, first_col_sum, zeros)
    for k in range(nk):
        total = jnp.sum(sums[k], axis=0, keepdims=True)
        col_s[0, me_s, :, chunk(k)] = peaks[k] + jnp.log2(total)
    col_lse = col_reduce(0, lse2)
    g_first = warm2 - math.log2(cols_all) - col_lse
    local_weight = jnp.concatenate(
        [
            jnp.exp2(peaks[k] - col_lse[:, k * L : (k + 1) * L] - math.log2(cols_all))
            for k in range(nk)
        ],
        axis=1,
    )

    def row_pass(weight):
        weights = [weight[:, k * L : (k + 1) * L] for k in range(nk)]

        def body(a, acc):
            total = e_f32[a, :, chunk(0)] * weights[0]
            for k in range(1, nk):
                total = total + e_f32[a, :, chunk(k)] * weights[k]
            total = jnp.sum(total, axis=1, keepdims=True)
            return jnp.where(lane == a, total, acc)

        return lax.fori_loop(0, nb, body, zero_tile, unroll=2)

    def col_pass(index):
        def body(a, accs):
            u_col = column_of(a)
            return tuple(
                accs[k] + fold(e_f32[a, :, chunk(k)] * u_col, jnp.add) for k in range(nk)
            )

        sums = lax.fori_loop(0, nb, body, zeros, unroll=2)
        for k in range(nk):
            total = jnp.sum(sums[k], axis=0, keepdims=True)
            col_s[index, me_s, :, chunk(k)] = total * local_weight[:, k * L : (k + 1) * L]

    weight = local_weight
    v_val = None
    for index in range(1, ROUNDS):
        mass = row_reduce(index, row_pass(weight), total_of)
        spread(1.0 / (mass * rows_all))
        col_pass(index)
        v_val = 1.0 / (col_reduce(index, total_of) * cols_all)
        weight = local_weight * v_val

    def barycentric():
        col_out[...] = (EPS * LN2) * (g_first + jnp.log2(v_val))
        pieces = [split(tgt_t[k] * weight[:, k * L : (k + 1) * L]) for k in range(nk)]
        both = jnp.concatenate(
            [
                jnp.concatenate([p[0] for p in pieces], axis=1),
                jnp.concatenate([p[1] for p in pieces], axis=1),
            ],
            axis=0,
        )

        def body(a, carry):
            block = e_b16[pl.ds(a * 4, 4)].reshape(4 * L, cols)
            out = dot_nt(block, both)
            high, low = split(out[:, :width] + out[:, width:])
            start = pl.multiple_of(a * 4 * L, 4 * L)
            bary[pl.ds(start, 4 * L), pl.ds(0, width)] = high
            bary[pl.ds(start, 4 * L), pl.ds(width, width)] = low
            return carry

        lax.fori_loop(0, nb // 4, body, 0)

    mass = row_reduce(ROUNDS, row_pass(weight), total_of, barycentric)
    row_out[...] = (EPS * LN2) * (f_first - math.log2(rows_all) - jnp.log2(mass))
    inverse = 1.0 / mass

    pieces = [split(src_t[a] * inverse[a : a + 1, :]) for a in range(nb)]
    stacked = jnp.concatenate(
        [
            jnp.concatenate([p[0] for p in pieces], axis=1),
            jnp.concatenate([p[1] for p in pieces], axis=1),
        ],
        axis=0,
    )
    out = dot_nn(stacked, bary[...])
    cross[...] = (
        out[:width, :width] + out[:width, width:] + out[width:, :width] + out[width:, width:]
    ).reshape(NSRC, width // NSRC, width)

    phase = 3 * ROUNDS + 2
    cross_s[me_s] = cross[me_s]
    for peer in peers_s:
        pltpu.make_async_remote_copy(
            src_ref=cross.at[peer[0]],
            dst_ref=cross_s.at[me_s],
            send_sem=send_sem.at[phase],
            recv_sem=recv_sem.at[phase],
            device_id=peer,
            device_id_type=MESH,
        ).start()
    others = cross_s.at[pl.ds(0, len(peers_s))]
    done = pltpu.make_async_remote_copy(
        src_ref=others,
        dst_ref=others,
        send_sem=send_sem.at[phase],
        recv_sem=recv_sem.at[phase],
        device_id=peers_s[0],
        device_id_type=MESH,
    )
    pending.append(done)
    done.wait_recv()
    cross_z[me_z] = total_of([cross_s[i] for i in range(NSRC)])
    send(phase + 1, cross_z, me_z, peers_z).wait_recv()
    cross_x[me_x] = total_of([cross_z[i] for i in range(NZ)])
    send(phase + 2, cross_x, me_x, peers_x).wait_recv()
    cross_g[me_s] = total_of([cross_x[i] for i in range(NX)])
    send(phase + 3, cross_g, me_s, peers_s).wait_recv()

    matrix = cross_g[...].reshape(width, width)
    norm = jnp.sum(jnp.sum(matrix * matrix, axis=1, keepdims=True), axis=0, keepdims=True)
    iterate = matrix / jnp.sqrt(norm + 1e-06)

    def newton(_, iterate):
        high, low = split(iterate)
        pair = jnp.concatenate([high, low], axis=1)
        twice = jnp.concatenate(
            [jnp.concatenate([high, high], axis=1), jnp.concatenate([low, low], axis=1)], axis=0
        )
        gram = dot_nt(pair, twice)
        gram = gram[:, :width] + gram[:, width:]
        pair_g = jnp.concatenate(split(gram), axis=1)
        stack = jnp.concatenate([pair, pair], axis=0)
        prod = dot_nn(pair_g, stack)
        return 1.5 * iterate - 0.5 * (prod[:, :width] + prod[:, width:])

    map_out[...] = lax.fori_loop(0, NEWTON, newton, iterate)
    for done in pending:
        done.wait_send()


def shards(source, target, start_map, warm_potential):
    rows, width = source.shape
    cols = target.shape[0]
    rows_all, cols_all = rows * lax.axis_size("src"), cols * lax.axis_size("tgt")
    nb, nk = rows // L, cols // L
    phases = 3 * ROUNDS + 2 + 4
    vmem = pltpu.VMEM
    row_pot, col_pot, new_map = pl.pallas_call(
        functools.partial(kernel, rows_all, cols_all),
        out_shape=(
            jax.ShapeDtypeStruct((nb, L), F32),
            jax.ShapeDtypeStruct((1, cols), F32),
            jax.ShapeDtypeStruct((width, width), F32),
        ),
        in_specs=[pl.BlockSpec(memory_space=vmem)] * 4,
        out_specs=[pl.BlockSpec(memory_space=vmem)] * 3,
        scratch_shapes=[
            vmem((rows, width), BF16),
            vmem((nb, L, cols), F32),
            vmem((nb, L, cols), BF16),
            vmem((nb, width, L), F32),
            vmem((nk, width, L), F32),
            vmem((rows, 2 * width), BF16),
            vmem((L, L), F32),
            vmem((NSRC, width // NSRC, width), F32),
            vmem((ROUNDS + 1, NZ, nb, L), F32),
            vmem((ROUNDS + 1, NX, nb, L), F32),
            vmem((ROUNDS, NSRC, 1, cols), F32),
            vmem((NSRC, width // NSRC, width), F32),
            vmem((NZ, width // NSRC, width), F32),
            vmem((NX, width // NSRC, width), F32),
            vmem((NSRC, width // NSRC, width), F32),
            pltpu.SemaphoreType.DMA((phases,)),
            pltpu.SemaphoreType.DMA((phases,)),
        ],
        compiler_params=pltpu.CompilerParams(
            collective_id=0, has_side_effects=True, vmem_limit_bytes=48 << 20
        ),
        name="sinkhorn_refit",
    )(source, target, start_map, warm_potential.reshape(1, cols))
    return row_pot.reshape(rows), col_pot.reshape(cols), new_map


def solution(mesh):
    placed = (P("src", None), P("tgt", None), P(), P("tgt"))
    return jax.shard_map(
        shards,
        mesh=mesh,
        in_specs=placed,
        out_specs=(P("src"), P("tgt"), P()),
        check_vma=False,
    )
```

```python
import functools
import math

import jax
import jax.numpy as jnp
from jax import lax
from jax.experimental import pallas as pl
from jax.experimental.pallas import tpu as pltpu
from jax.sharding import PartitionSpec as P

ROUNDS = 3
NEWTON = 10
EPS = 0.05
LN2 = math.log(2.0)
MESH = pl.DeviceIdType.MESH
F32 = jnp.float32
BF16 = jnp.bfloat16
NX, NY, NZ, NC = 4, 4, 8, 2
NSRC = NY * NC
L = 128


def split(value):
    high = value.astype(BF16)
    low = (value - high.astype(F32)).astype(BF16)
    return high, low


def dot_nt(a, b):
    return lax.dot_general(a, b, (((1,), (1,)), ((), ())), preferred_element_type=F32)


def dot_nn(a, b):
    return jnp.dot(a, b, preferred_element_type=F32)


def lse2(parts):
    peak = parts[0]
    for part in parts[1:]:
        peak = jnp.maximum(peak, part)
    total = jnp.exp2(parts[0] - peak)
    for part in parts[1:]:
        total = total + jnp.exp2(part - peak)
    return peak + jnp.log2(total)


def total_of(parts):
    total = parts[0]
    for part in parts[1:]:
        total = total + part
    return total


def kernel(
    rows_all,
    cols_all,
    source_hbm,
    target_hbm,
    map_hbm,
    warm_hbm,
    row_out,
    col_out,
    cross_g,
    source_ref,
    target_ref,
    map_ref,
    warm_ref,
    rot,
    e_f32,
    e_b16,
    src_t,
    tgt_t,
    bary,
    u_t,
    cross,
    row_z,
    row_x,
    col_s,
    cross_s,
    cross_z,
    cross_x,
    send_sem,
    recv_sem,
    load_sem,
):
    loads = [
        pltpu.make_async_copy(hbm, ref, load_sem.at[i])
        for i, (hbm, ref) in enumerate(
            [
                (map_hbm, map_ref),
                (source_hbm, source_ref),
                (target_hbm, target_ref),
                (warm_hbm, warm_ref),
            ]
        )
    ]
    for load in loads:
        load.start()
    rows, width = source_ref.shape
    cols = target_ref.shape[0]
    nb, nk = rows // L, cols // L
    scale2 = 1.0 / (math.sqrt(width) * EPS) / LN2
    me_s = lax.axis_index("src")
    me_t = lax.axis_index("tgt")
    me_x, me_z = me_t // NZ, lax.rem(me_t, NZ)
    peers_s = [(lax.rem(me_s + k, NSRC), me_t) for k in (4, 3, 5, 2, 6, 1, 7)]
    peers_z = [(me_s, me_x * NZ + lax.rem(me_z + k, NZ)) for k in (4, 3, 5, 2, 6, 1, 7)]
    peers_x = [(me_s, lax.rem(me_x + k, NX) * NZ + me_z) for k in (2, 1, 3)]

    barrier = pltpu.get_barrier_semaphore()
    everyone = peers_s + peers_z + peers_x
    for peer in everyone:
        pl.semaphore_signal(barrier, inc=1, device_id=peer, device_id_type=MESH)

    pending = []

    def send(phase, buf, me, peers):
        for peer in peers:
            pltpu.make_async_remote_copy(
                src_ref=buf.at[me],
                dst_ref=buf.at[me],
                send_sem=send_sem.at[phase],
                recv_sem=recv_sem.at[phase],
                device_id=peer,
                device_id_type=MESH,
            ).start()
        others = buf.at[pl.ds(0, len(peers))]
        done = pltpu.make_async_remote_copy(
            src_ref=others,
            dst_ref=others,
            send_sem=send_sem.at[phase],
            recv_sem=recv_sem.at[phase],
            device_id=peers[0],
            device_id_type=MESH,
        )
        pending.append(done)
        return done

    lane = lax.broadcasted_iota(jnp.int32, (L, L), 1)
    zero_tile = jnp.zeros((L, L), F32)

    def chunk(k):
        return pl.ds(k * L, L)

    loads[0].wait()
    loads[1].wait()
    rot[...] = dot_nn(source_ref[...], map_ref[...].astype(BF16)).astype(BF16)
    loads[2].wait()
    loads[3].wait()
    warm2 = warm_ref[...] * (1.0 / LN2)
    wide = 256
    for k in range(cols // wide):
        part = target_ref[pl.ds(k * wide, wide), :]
        warm_part = warm2[:, k * wide : (k + 1) * wide]

        def score_block(a, carry):
            block = rot[pl.ds(pl.multiple_of(a * 512, 512), 512), :]
            e_f32[pl.ds(a * 4, 4), :, pl.ds(k * wide, wide)] = (
                dot_nt(block, part) * scale2 + warm_part
            ).reshape(4, L, wide)
            return carry

        lax.fori_loop(0, rows // 512, score_block, 0, unroll=4)

    def first_row(a, acc):
        peak = e_f32[a, :, chunk(0)]
        for k in range(1, nk):
            peak = jnp.maximum(peak, e_f32[a, :, chunk(k)])
        peak = jnp.max(peak, axis=1, keepdims=True)
        total = jnp.exp2(e_f32[a, :, chunk(0)] - peak)
        for k in range(1, nk):
            total = total + jnp.exp2(e_f32[a, :, chunk(k)] - peak)
        total = jnp.sum(total, axis=1, keepdims=True)
        return jnp.where(lane == a, peak + jnp.log2(total), acc)

    first = lax.fori_loop(0, nb, first_row, zero_tile, unroll=4)
    pl.semaphore_wait(barrier, len(everyone))

    def row_reduce(index, tile, combine, meanwhile=None, meanwhile2=None):
        row_z[index, me_z] = tile.T[:nb]
        done = send(3 * index, row_z.at[index], me_z, peers_z)
        if meanwhile is not None:
            meanwhile()
        done.wait_recv()
        row_x[index, me_x] = combine([row_z[index, i] for i in range(NZ)])
        done = send(3 * index + 1, row_x.at[index], me_x, peers_x)
        if meanwhile2 is not None:
            meanwhile2()
        done.wait_recv()
        return combine([row_x[index, i] for i in range(NX)])

    def col_reduce(index, combine):
        done = send(3 * index + 2, col_s.at[index], me_s, peers_s)
        done.wait_recv()
        return combine([col_s[index, i] for i in range(NSRC)])

    def spread(value):
        u_t[...] = jnp.concatenate([value, jnp.zeros((L - nb, L), F32)], axis=0).T

    def column_of(a):
        return jnp.sum(jnp.where(lane == a, u_t[...], 0.0), axis=1, keepdims=True)

    def fold(tile, op):
        parts = [tile[8 * i : 8 * i + 8] for i in range(L // 8)]
        while len(parts) > 1:
            parts = [op(parts[i], parts[i + 1]) for i in range(0, len(parts), 2)]
        return parts[0]

    def transposes():
        def one_source(a, carry):
            block = source_ref[pl.ds(pl.multiple_of(a * L, L), L), :].astype(F32)
            src_t[a] = block.T
            return carry

        lax.fori_loop(0, nb, one_source, 0)

        def one_target(a, carry):
            block = target_ref[pl.ds(pl.multiple_of(a * L, L), L), :].astype(F32)
            tgt_t[a] = block.T
            return carry

        lax.fori_loop(0, nk, one_target, 0)

    row_lse = row_reduce(0, first, lse2, transposes)
    f_first = -math.log2(rows_all) - row_lse
    spread(f_first)

    def first_col_peak(a, accs):
        f_col = column_of(a)
        return tuple(
            jnp.maximum(accs[k], fold(e_f32[a, :, chunk(k)] + f_col, jnp.maximum))
            for k in range(nk)
        )

    peaks = lax.fori_loop(
        0, nb, first_col_peak, tuple(jnp.full((8, L), -jnp.inf, F32) for _ in range(nk)), unroll=8
    )
    peaks = [jnp.max(p, axis=0, keepdims=True) for p in peaks]

    def first_col_sum(a, accs):
        f_col = column_of(a)
        out = []
        for k in range(nk):
            e_val = jnp.exp2((e_f32[a, :, chunk(k)] + f_col) - peaks[k])
            e_f32[a, :, chunk(k)] = e_val
            e_b16[a, :, chunk(k)] = e_val.astype(BF16)
            out.append(accs[k] + fold(e_val, jnp.add))
        return tuple(out)

    zeros = tuple(jnp.zeros((8, L), F32) for _ in range(nk))
    sums = lax.fori_loop(0, nb, first_col_sum, zeros, unroll=4)
    for k in range(nk):
        total = jnp.sum(sums[k], axis=0, keepdims=True)
        col_s[0, me_s, :, chunk(k)] = peaks[k] + jnp.log2(total)
    col_lse = col_reduce(0, lse2)
    g_first = warm2 - math.log2(cols_all) - col_lse
    local_weight = jnp.concatenate(
        [
            jnp.exp2(peaks[k] - col_lse[:, k * L : (k + 1) * L] - math.log2(cols_all))
            for k in range(nk)
        ],
        axis=1,
    )

    def row_pass(weight):
        weights = [weight[:, k * L : (k + 1) * L] for k in range(nk)]

        def body(a, acc):
            total = e_f32[a, :, chunk(0)] * weights[0]
            for k in range(1, nk):
                total = total + e_f32[a, :, chunk(k)] * weights[k]
            total = jnp.sum(total, axis=1, keepdims=True)
            return jnp.where(lane == a, total, acc)

        return lax.fori_loop(0, nb, body, zero_tile, unroll=16)

    def col_pass(index):
        def body(a, accs):
            u_col = column_of(a)
            return tuple(
                accs[k] + fold(e_f32[a, :, chunk(k)] * u_col, jnp.add) for k in range(nk)
            )

        sums = lax.fori_loop(0, nb, body, zeros, unroll=16)
        for k in range(nk):
            total = jnp.sum(sums[k], axis=0, keepdims=True)
            col_s[index, me_s, :, chunk(k)] = total * local_weight[:, k * L : (k + 1) * L]

    weight = local_weight
    v_val = None
    for index in range(1, ROUNDS):
        mass = row_reduce(index, row_pass(weight), total_of)
        spread(1.0 / (mass * rows_all))
        col_pass(index)
        v_val = 1.0 / (col_reduce(index, total_of) * cols_all)
        weight = local_weight * v_val

    def barycentric():
        col_out[...] = (EPS * LN2) * (g_first + jnp.log2(v_val))
        pieces = [split(tgt_t[k] * weight[:, k * L : (k + 1) * L]) for k in range(nk)]
        both = jnp.concatenate(
            [
                jnp.concatenate([p[0] for p in pieces], axis=1),
                jnp.concatenate([p[1] for p in pieces], axis=1),
            ],
            axis=0,
        )

        def body(a, carry):
            block = e_b16[pl.ds(a * 4, 4)].reshape(4 * L, cols)
            out = dot_nt(block, both)
            high, low = split(out[:, :width] + out[:, width:])
            start = pl.multiple_of(a * 4 * L, 4 * L)
            bary[pl.ds(start, 4 * L), pl.ds(0, width)] = high
            bary[pl.ds(start, 4 * L), pl.ds(width, width)] = low
            return carry

        lax.fori_loop(0, nb // 4, body, 0, unroll=2)

    mass = row_reduce(ROUNDS, row_pass(weight), total_of, barycentric)
    row_out[...] = (EPS * LN2) * (f_first - math.log2(rows_all) - jnp.log2(mass))
    inverse = 1.0 / mass

    pieces = [split(src_t[a] * inverse[a : a + 1, :]) for a in range(nb)]
    stacked = jnp.concatenate(
        [
            jnp.concatenate([p[0] for p in pieces], axis=1),
            jnp.concatenate([p[1] for p in pieces], axis=1),
        ],
        axis=0,
    )
    out = dot_nn(stacked, bary[...])
    cross[...] = (
        out[:width, :width] + out[:width, width:] + out[width:, :width] + out[width:, width:]
    ).reshape(NSRC, width // NSRC, width)

    phase = 3 * ROUNDS + 2
    cross_s[me_s] = cross[me_s]
    for peer in peers_s:
        pltpu.make_async_remote_copy(
            src_ref=cross.at[peer[0]],
            dst_ref=cross_s.at[me_s],
            send_sem=send_sem.at[phase],
            recv_sem=recv_sem.at[phase],
            device_id=peer,
            device_id_type=MESH,
        ).start()
    others = cross_s.at[pl.ds(0, len(peers_s))]
    done = pltpu.make_async_remote_copy(
        src_ref=others,
        dst_ref=others,
        send_sem=send_sem.at[phase],
        recv_sem=recv_sem.at[phase],
        device_id=peers_s[0],
        device_id_type=MESH,
    )
    pending.append(done)
    done.wait_recv()
    cross_z[me_z] = total_of([cross_s[i] for i in range(NSRC)])
    send(phase + 1, cross_z, me_z, peers_z).wait_recv()
    cross_x[me_x] = total_of([cross_z[i] for i in range(NZ)])
    send(phase + 2, cross_x, me_x, peers_x).wait_recv()
    cross_g[me_s] = total_of([cross_x[i] for i in range(NX)])
    send(phase + 3, cross_g, me_s, peers_s).wait_recv()

    for done in pending:
        done.wait_send()


def polar_kernel(cross_ref, row_ref, col_ref, row_out, col_out, map_out, result, sems):
    stores = [
        pltpu.make_async_copy(row_ref, row_out, sems.at[0]),
        pltpu.make_async_copy(col_ref, col_out, sems.at[1]),
        pltpu.make_async_copy(result, map_out, sems.at[2]),
    ]
    stores[0].start()
    stores[1].start()
    width = result.shape[0]
    matrix = cross_ref[...].reshape(width, width)
    norm = jnp.sum(jnp.sum(matrix * matrix, axis=1, keepdims=True), axis=0, keepdims=True)
    iterate = matrix / jnp.sqrt(norm + 1e-06)

    def newton(_, iterate):
        high, low = split(iterate)
        pair = jnp.concatenate([high, low], axis=1)
        twice = jnp.concatenate(
            [jnp.concatenate([high, high], axis=1), jnp.concatenate([low, low], axis=1)], axis=0
        )
        gram = dot_nt(pair, twice)
        gram = gram[:, :width] + gram[:, width:]
        pair_g = jnp.concatenate(split(gram), axis=1)
        stack = jnp.concatenate([pair, pair], axis=0)
        prod = dot_nn(pair_g, stack)
        return 1.5 * iterate - 0.5 * (prod[:, :width] + prod[:, width:])

    result[...] = lax.fori_loop(0, NEWTON, newton, iterate)
    stores[2].start()
    for store in stores:
        store.wait()


def shards(source, target, start_map, warm_potential):
    rows, width = source.shape
    cols = target.shape[0]
    rows_all, cols_all = rows * lax.axis_size("src"), cols * lax.axis_size("tgt")
    nb, nk = rows // L, cols // L
    phases = 3 * ROUNDS + 2 + 4
    vmem = pltpu.VMEM
    pots = (jax.ShapeDtypeStruct((nb, L), F32), jax.ShapeDtypeStruct((1, cols), F32))
    part_shape = (NSRC, width // NSRC, width)
    row_pot, col_pot, cross = pl.pallas_call(
        functools.partial(kernel, rows_all, cols_all),
        out_shape=(*pots, jax.ShapeDtypeStruct(part_shape, F32)),
        in_specs=[pl.BlockSpec(memory_space=pl.ANY)] * 4,
        out_specs=[pl.BlockSpec(memory_space=vmem)] * 3,
        scratch_shapes=[
            vmem((rows, width), BF16),
            vmem((cols, width), BF16),
            vmem((width, width), F32),
            vmem((1, cols), F32),
            vmem((rows, width), BF16),
            vmem((nb, L, cols), F32),
            vmem((nb, L, cols), BF16),
            vmem((nb, width, L), F32),
            vmem((nk, width, L), F32),
            vmem((rows, 2 * width), BF16),
            vmem((L, L), F32),
            vmem(part_shape, F32),
            vmem((ROUNDS + 1, NZ, nb, L), F32),
            vmem((ROUNDS + 1, NX, nb, L), F32),
            vmem((ROUNDS, NSRC, 1, cols), F32),
            vmem(part_shape, F32),
            vmem((NZ, *part_shape[1:]), F32),
            vmem((NX, *part_shape[1:]), F32),
            pltpu.SemaphoreType.DMA((phases,)),
            pltpu.SemaphoreType.DMA((phases,)),
            pltpu.SemaphoreType.DMA((4,)),
        ],
        compiler_params=pltpu.CompilerParams(
            collective_id=0, has_side_effects=True, vmem_limit_bytes=60 << 20
        ),
        name="sinkhorn",
    )(source, target, start_map, warm_potential.reshape(1, cols))
    row_pot, col_pot, new_map = pl.pallas_call(
        polar_kernel,
        out_shape=(*pots, jax.ShapeDtypeStruct((width, width), F32)),
        in_specs=[pl.BlockSpec(memory_space=vmem)] * 3,
        out_specs=[pl.BlockSpec(memory_space=pl.ANY)] * 3,
        scratch_shapes=[vmem((width, width), F32), pltpu.SemaphoreType.DMA((3,))],
        name="polar",
    )(cross, row_pot, col_pot)
    return row_pot.reshape(rows), col_pot.reshape(cols), new_map


def solution(mesh):
    placed = (P("src", None), P("tgt", None), P(), P("tgt"))
    return jax.shard_map(
        shards,
        mesh=mesh,
        in_specs=placed,
        out_specs=(P("src"), P("tgt"), P()),
        check_vma=False,
    )
```

```python
import functools
import math

import jax
import jax.numpy as jnp
from jax import lax
from jax.experimental import pallas as pl
from jax.experimental.pallas import tpu as pltpu
from jax.sharding import PartitionSpec as P

ROUNDS = 3
NEWTON = 10
EPS = 0.05
LN2 = math.log(2.0)
MESH = pl.DeviceIdType.MESH
F32 = jnp.float32
BF16 = jnp.bfloat16
NX, NY, NZ, NC = 4, 4, 8, 2
NSRC = NY * NC
NPART = NSRC * NX
L = 128


def split(value):
    high = value.astype(BF16)
    low = (value - high.astype(F32)).astype(BF16)
    return high, low


def dot_nt(a, b):
    return lax.dot_general(a, b, (((1,), (1,)), ((), ())), preferred_element_type=F32)


def dot_nn(a, b):
    return jnp.dot(a, b, preferred_element_type=F32)


def lse2(parts):
    peak = parts[0]
    for part in parts[1:]:
        peak = jnp.maximum(peak, part)
    total = jnp.exp2(parts[0] - peak)
    for part in parts[1:]:
        total = total + jnp.exp2(part - peak)
    return peak + jnp.log2(total)


def total_of(parts):
    total = parts[0]
    for part in parts[1:]:
        total = total + part
    return total


def kernel(
    rows_all,
    cols_all,
    source_hbm,
    target_hbm,
    map_hbm,
    warm_hbm,
    row_out,
    col_out,
    cross_g,
    source_ref,
    target_ref,
    map_ref,
    warm_ref,
    rot,
    e_f32,
    e_b16,
    src_t,
    tgt_t,
    bary,
    u_t,
    cross,
    row_z,
    row_x,
    col_s,
    cross_p,
    cross_z,
    send_sem,
    recv_sem,
    load_sem,
):
    loads = [
        pltpu.make_async_copy(hbm, ref, load_sem.at[i])
        for i, (hbm, ref) in enumerate(
            [
                (map_hbm, map_ref),
                (source_hbm, source_ref),
                (target_hbm, target_ref),
                (warm_hbm, warm_ref),
            ]
        )
    ]
    for load in loads:
        load.start()
    rows, width = source_ref.shape
    cols = target_ref.shape[0]
    nb, nk = rows // L, cols // L
    scale2 = 1.0 / (math.sqrt(width) * EPS) / LN2
    me_s = lax.axis_index("src")
    me_t = lax.axis_index("tgt")
    me_x, me_z = me_t // NZ, lax.rem(me_t, NZ)
    peers_s = [(lax.rem(me_s + k, NSRC), me_t) for k in (4, 3, 5, 2, 6, 1, 7)]
    peers_z = [(me_s, me_x * NZ + lax.rem(me_z + k, NZ)) for k in (4, 3, 5, 2, 6, 1, 7)]
    peers_x = [(me_s, lax.rem(me_x + k, NX) * NZ + me_z) for k in (2, 1, 3)]

    me_p = me_s * NX + me_x
    peers_p = [
        (lax.rem(me_s + b, NSRC), lax.rem(me_x + a, NX) * NZ + me_z)
        for a in (2, 1, 3, 0)
        for b in (4, 3, 5, 2, 6, 1, 7, 0)
        if a or b
    ]

    barrier = pltpu.get_barrier_semaphore()
    everyone = peers_z + peers_p
    for peer in everyone:
        pl.semaphore_signal(barrier, inc=1, device_id=peer, device_id_type=MESH)

    pending = []

    def send(phase, buf, me, peers):
        for peer in peers:
            pltpu.make_async_remote_copy(
                src_ref=buf.at[me],
                dst_ref=buf.at[me],
                send_sem=send_sem.at[phase],
                recv_sem=recv_sem.at[phase],
                device_id=peer,
                device_id_type=MESH,
            ).start()
        others = buf.at[pl.ds(0, len(peers))]
        done = pltpu.make_async_remote_copy(
            src_ref=others,
            dst_ref=others,
            send_sem=send_sem.at[phase],
            recv_sem=recv_sem.at[phase],
            device_id=peers[0],
            device_id_type=MESH,
        )
        pending.append(done)
        return done

    lane = lax.broadcasted_iota(jnp.int32, (L, L), 1)
    zero_tile = jnp.zeros((L, L), F32)

    def chunk(k):
        return pl.ds(k * L, L)

    loads[0].wait()
    loads[1].wait()
    rot[...] = dot_nn(source_ref[...], map_ref[...].astype(BF16)).astype(BF16)
    loads[2].wait()
    loads[3].wait()
    warm2 = warm_ref[...] * (1.0 / LN2)
    wide = 256
    for k in range(cols // wide):
        part = target_ref[pl.ds(k * wide, wide), :]
        warm_part = warm2[:, k * wide : (k + 1) * wide]

        def score_block(a, carry):
            block = rot[pl.ds(pl.multiple_of(a * 512, 512), 512), :]
            e_f32[pl.ds(a * 4, 4), :, pl.ds(k * wide, wide)] = (
                dot_nt(block, part) * scale2 + warm_part
            ).reshape(4, L, wide)
            return carry

        lax.fori_loop(0, rows // 512, score_block, 0, unroll=4)

    def first_row(a, acc):
        peak = e_f32[a, :, chunk(0)]
        for k in range(1, nk):
            peak = jnp.maximum(peak, e_f32[a, :, chunk(k)])
        peak = jnp.max(peak, axis=1, keepdims=True)
        total = jnp.exp2(e_f32[a, :, chunk(0)] - peak)
        for k in range(1, nk):
            total = total + jnp.exp2(e_f32[a, :, chunk(k)] - peak)
        total = jnp.sum(total, axis=1, keepdims=True)
        return jnp.where(lane == a, peak + jnp.log2(total), acc)

    first = lax.fori_loop(0, nb, first_row, zero_tile, unroll=4)
    pl.semaphore_wait(barrier, len(everyone))

    def row_reduce(index, tile, combine, meanwhile=None, meanwhile2=None):
        row_z[index, me_z] = tile.T[:nb]
        done = send(3 * index, row_z.at[index], me_z, peers_z)
        if meanwhile is not None:
            meanwhile()
        done.wait_recv()
        row_x[index, me_x] = combine([row_z[index, i] for i in range(NZ)])
        done = send(3 * index + 1, row_x.at[index], me_x, peers_x)
        if meanwhile2 is not None:
            meanwhile2()
        done.wait_recv()
        return combine([row_x[index, i] for i in range(NX)])

    def col_reduce(index, combine, meanwhile=None):
        done = send(3 * index + 2, col_s.at[index], me_s, peers_s)
        if meanwhile is not None:
            meanwhile()
        done.wait_recv()
        return combine([col_s[index, i] for i in range(NSRC)])

    def spread(value):
        u_t[...] = jnp.concatenate([value, jnp.zeros((L - nb, L), F32)], axis=0).T

    def column_of(a):
        return jnp.sum(jnp.where(lane == a, u_t[...], 0.0), axis=1, keepdims=True)

    def fold(tile, op):
        parts = [tile[8 * i : 8 * i + 8] for i in range(L // 8)]
        while len(parts) > 1:
            parts = [op(parts[i], parts[i + 1]) for i in range(0, len(parts), 2)]
        return parts[0]

    def transposes():
        def one_source(a, carry):
            block = source_ref[pl.ds(pl.multiple_of(a * L, L), L), :].astype(F32)
            src_t[a] = block.T
            return carry

        lax.fori_loop(0, nb, one_source, 0)

        def one_target(a, carry):
            block = target_ref[pl.ds(pl.multiple_of(a * L, L), L), :].astype(F32)
            tgt_t[a] = block.T
            return carry

        lax.fori_loop(0, nk, one_target, 0)

    row_lse = row_reduce(0, first, lse2, transposes)
    f_first = -math.log2(rows_all) - row_lse
    spread(f_first)

    def first_col_peak(a, accs):
        f_col = column_of(a)
        return tuple(
            jnp.maximum(accs[k], fold(e_f32[a, :, chunk(k)] + f_col, jnp.maximum))
            for k in range(nk)
        )

    peaks = lax.fori_loop(
        0, nb, first_col_peak, tuple(jnp.full((8, L), -jnp.inf, F32) for _ in range(nk)), unroll=8
    )
    peaks = [jnp.max(p, axis=0, keepdims=True) for p in peaks]

    def first_col_sum(a, accs):
        f_col = column_of(a)
        out = []
        for k in range(nk):
            e_val = jnp.exp2((e_f32[a, :, chunk(k)] + f_col) - peaks[k])
            e_f32[a, :, chunk(k)] = e_val
            out.append(accs[k] + fold(e_val, jnp.add))
        return tuple(out)

    zeros = tuple(jnp.zeros((8, L), F32) for _ in range(nk))
    sums = lax.fori_loop(0, nb, first_col_sum, zeros, unroll=4)
    for k in range(nk):
        total = jnp.sum(sums[k], axis=0, keepdims=True)
        col_s[0, me_s, :, chunk(k)] = peaks[k] + jnp.log2(total)

    def narrow():
        def body(a, carry):
            for k in range(nk):
                e_b16[a, :, chunk(k)] = e_f32[a, :, chunk(k)].astype(BF16)
            return carry

        lax.fori_loop(0, nb, body, 0)

    col_lse = col_reduce(0, lse2, narrow)
    g_first = warm2 - math.log2(cols_all) - col_lse
    local_weight = jnp.concatenate(
        [
            jnp.exp2(peaks[k] - col_lse[:, k * L : (k + 1) * L] - math.log2(cols_all))
            for k in range(nk)
        ],
        axis=1,
    )

    def row_pass(weight):
        weights = [weight[:, k * L : (k + 1) * L] for k in range(nk)]

        def body(a, acc):
            total = e_f32[a, :, chunk(0)] * weights[0]
            for k in range(1, nk):
                total = total + e_f32[a, :, chunk(k)] * weights[k]
            total = jnp.sum(total, axis=1, keepdims=True)
            return jnp.where(lane == a, total, acc)

        return lax.fori_loop(0, nb, body, zero_tile, unroll=16)

    def col_pass(index):
        def body(a, accs):
            u_col = column_of(a)
            return tuple(
                accs[k] + fold(e_f32[a, :, chunk(k)] * u_col, jnp.add) for k in range(nk)
            )

        sums = lax.fori_loop(0, nb, body, zeros, unroll=16)
        for k in range(nk):
            total = jnp.sum(sums[k], axis=0, keepdims=True)
            col_s[index, me_s, :, chunk(k)] = total * local_weight[:, k * L : (k + 1) * L]

    weight = local_weight
    v_val = None
    for index in range(1, ROUNDS):
        mass = row_reduce(index, row_pass(weight), total_of)
        spread(1.0 / (mass * rows_all))
        col_pass(index)
        v_val = 1.0 / (col_reduce(index, total_of) * cols_all)
        weight = local_weight * v_val

    def barycentric():
        col_out[...] = (EPS * LN2) * (g_first + jnp.log2(v_val))
        pieces = [split(tgt_t[k] * weight[:, k * L : (k + 1) * L]) for k in range(nk)]
        both = jnp.concatenate(
            [
                jnp.concatenate([p[0] for p in pieces], axis=1),
                jnp.concatenate([p[1] for p in pieces], axis=1),
            ],
            axis=0,
        )

        def body(a, carry):
            block = e_b16[pl.ds(a * 4, 4)].reshape(4 * L, cols)
            out = dot_nt(block, both)
            high, low = split(out[:, :width] + out[:, width:])
            start = pl.multiple_of(a * 4 * L, 4 * L)
            bary[pl.ds(start, 4 * L), pl.ds(0, width)] = high
            bary[pl.ds(start, 4 * L), pl.ds(width, width)] = low
            return carry

        lax.fori_loop(0, nb // 4, body, 0, unroll=2)

    mass = row_reduce(ROUNDS, row_pass(weight), total_of, barycentric)
    row_out[...] = (EPS * LN2) * (f_first - math.log2(rows_all) - jnp.log2(mass))
    inverse = 1.0 / mass

    pieces = [split(src_t[a] * inverse[a : a + 1, :]) for a in range(nb)]
    stacked = jnp.concatenate(
        [
            jnp.concatenate([p[0] for p in pieces], axis=1),
            jnp.concatenate([p[1] for p in pieces], axis=1),
        ],
        axis=0,
    )
    out = dot_nn(stacked, bary[...])
    cross[...] = (
        out[:width, :width] + out[:width, width:] + out[width:, :width] + out[width:, width:]
    ).reshape(NPART, width // NPART, width)

    phase = 3 * ROUNDS + 2
    cross_p[me_p] = cross[me_p]
    for peer in peers_p:
        pltpu.make_async_remote_copy(
            src_ref=cross.at[peer[0] * NX + peer[1] // NZ],
            dst_ref=cross_p.at[me_p],
            send_sem=send_sem.at[phase],
            recv_sem=recv_sem.at[phase],
            device_id=peer,
            device_id_type=MESH,
        ).start()
    others = cross_p.at[pl.ds(0, len(peers_p))]
    done = pltpu.make_async_remote_copy(
        src_ref=others,
        dst_ref=others,
        send_sem=send_sem.at[phase],
        recv_sem=recv_sem.at[phase],
        device_id=peers_p[0],
        device_id_type=MESH,
    )
    pending.append(done)
    done.wait_recv()
    cross_z[me_z] = jnp.sum(cross_p[...], axis=0)
    send(phase + 1, cross_z, me_z, peers_z).wait_recv()
    cross_g[me_p] = jnp.sum(cross_z[...], axis=0)
    send(phase + 2, cross_g, me_p, peers_p).wait_recv()

    for done in pending:
        done.wait_send()


def polar_kernel(cross_ref, row_ref, col_ref, row_out, col_out, map_out, result, sems):
    stores = [
        pltpu.make_async_copy(row_ref, row_out, sems.at[0]),
        pltpu.make_async_copy(col_ref, col_out, sems.at[1]),
        pltpu.make_async_copy(result, map_out, sems.at[2]),
    ]
    stores[0].start()
    stores[1].start()
    width = result.shape[0]
    matrix = cross_ref[...].reshape(width, width)
    norm = jnp.sum(jnp.sum(matrix * matrix, axis=1, keepdims=True), axis=0, keepdims=True)
    iterate = matrix / jnp.sqrt(norm + 1e-06)

    def newton(_, iterate):
        high, low = split(iterate)
        pair = jnp.concatenate([high, low], axis=1)
        twice = jnp.concatenate(
            [jnp.concatenate([high, high], axis=1), jnp.concatenate([low, low], axis=1)], axis=0
        )
        gram = dot_nt(pair, twice)
        gram = gram[:, :width] + gram[:, width:]
        pair_g = jnp.concatenate(split(gram), axis=1)
        stack = jnp.concatenate([pair, pair], axis=0)
        prod = dot_nn(pair_g, stack)
        return 1.5 * iterate - 0.5 * (prod[:, :width] + prod[:, width:])

    result[...] = lax.fori_loop(0, NEWTON, newton, iterate, unroll=10)
    stores[2].start()
    for store in stores:
        store.wait()


def shards(source, target, start_map, warm_potential):
    rows, width = source.shape
    cols = target.shape[0]
    rows_all, cols_all = rows * lax.axis_size("src"), cols * lax.axis_size("tgt")
    nb, nk = rows // L, cols // L
    phases = 3 * ROUNDS + 2 + 3
    vmem = pltpu.VMEM
    pots = (jax.ShapeDtypeStruct((nb, L), F32), jax.ShapeDtypeStruct((1, cols), F32))
    part_shape = (NPART, width // NPART, width)
    row_pot, col_pot, cross = pl.pallas_call(
        functools.partial(kernel, rows_all, cols_all),
        out_shape=(*pots, jax.ShapeDtypeStruct(part_shape, F32)),
        in_specs=[pl.BlockSpec(memory_space=pltpu.HBM)] * 4,
        out_specs=[pl.BlockSpec(memory_space=vmem)] * 3,
        scratch_shapes=[
            vmem((rows, width), BF16),
            vmem((cols, width), BF16),
            vmem((width, width), F32),
            vmem((1, cols), F32),
            vmem((rows, width), BF16),
            vmem((nb, L, cols), F32),
            vmem((nb, L, cols), BF16),
            vmem((nb, width, L), F32),
            vmem((nk, width, L), F32),
            vmem((rows, 2 * width), BF16),
            vmem((L, L), F32),
            vmem(part_shape, F32),
            vmem((ROUNDS + 1, NZ, nb, L), F32),
            vmem((ROUNDS + 1, NX, nb, L), F32),
            vmem((ROUNDS, NSRC, 1, cols), F32),
            vmem(part_shape, F32),
            vmem((NZ, *part_shape[1:]), F32),
            pltpu.SemaphoreType.DMA((phases,)),
            pltpu.SemaphoreType.DMA((phases,)),
            pltpu.SemaphoreType.DMA((4,)),
        ],
        compiler_params=pltpu.CompilerParams(
            collective_id=0, has_side_effects=True, vmem_limit_bytes=40 << 20
        ),
        name="sinkhorn",
    )(
        *(
            pltpu.with_memory_space_constraint(arg, pltpu.HBM)
            for arg in (source, target, start_map, warm_potential.reshape(1, cols))
        )
    )
    row_pot, col_pot, new_map = pl.pallas_call(
        polar_kernel,
        out_shape=(*pots, jax.ShapeDtypeStruct((width, width), F32)),
        in_specs=[pl.BlockSpec(memory_space=vmem)] * 3,
        out_specs=[pl.BlockSpec(memory_space=pltpu.HBM)] * 3,
        scratch_shapes=[vmem((width, width), F32), pltpu.SemaphoreType.DMA((3,))],
        compiler_params=pltpu.CompilerParams(vmem_limit_bytes=8 << 20),
        name="polar",
    )(cross, row_pot, col_pot)
    return row_pot.reshape(rows), col_pot.reshape(cols), new_map


def solution(mesh):
    placed = (P("src", None), P("tgt", None), P(), P("tgt"))
    return jax.shard_map(
        shards,
        mesh=mesh,
        in_specs=placed,
        out_specs=(P("src"), P("tgt"), P()),
        check_vma=False,
    )
```

```python
import functools
import math

import jax
import jax.numpy as jnp
from jax import lax
from jax.experimental import pallas as pl
from jax.experimental.pallas import tpu as pltpu
from jax.sharding import PartitionSpec as P

ROUNDS = 3
NEWTON = 10
EPS = 0.05
LN2 = math.log(2.0)
MESH = pl.DeviceIdType.MESH
F32 = jnp.float32
BF16 = jnp.bfloat16
NX, NY, NZ, NC = 4, 4, 8, 2
NSRC = NY * NC
NPART = NSRC * NX
HALVES = 2
ROW_PHASES = 2 * HALVES * (ROUNDS + 1)
L = 128


def split(value):
    high = value.astype(BF16)
    low = (value - high.astype(F32)).astype(BF16)
    return high, low


def dot_nt(a, b):
    return lax.dot_general(a, b, (((1,), (1,)), ((), ())), preferred_element_type=F32)


def dot_nn(a, b):
    return jnp.dot(a, b, preferred_element_type=F32)


def lse2(parts):
    peak = parts[0]
    for part in parts[1:]:
        peak = jnp.maximum(peak, part)
    total = jnp.exp2(parts[0] - peak)
    for part in parts[1:]:
        total = total + jnp.exp2(part - peak)
    return peak + jnp.log2(total)


def total_of(parts):
    total = parts[0]
    for part in parts[1:]:
        total = total + part
    return total


def kernel(
    rows_all,
    cols_all,
    source_hbm,
    target_hbm,
    map_hbm,
    warm_hbm,
    row_out,
    col_out,
    cross_g,
    source_ref,
    target_ref,
    map_ref,
    warm_ref,
    rot,
    e_f32,
    e_b16,
    src_t,
    tgt_t,
    bary,
    u_t,
    cross,
    row_z,
    row_x,
    col_s,
    cross_p,
    cross_z,
    send_sem,
    recv_sem,
    load_sem,
):
    loads = [
        pltpu.make_async_copy(hbm, ref, load_sem.at[i])
        for i, (hbm, ref) in enumerate(
            [
                (map_hbm, map_ref),
                (source_hbm, source_ref),
                (target_hbm, target_ref),
                (warm_hbm, warm_ref),
            ]
        )
    ]
    for load in loads:
        load.start()
    rows, width = source_ref.shape
    cols = target_ref.shape[0]
    nb, nk = rows // L, cols // L
    hb = nb // HALVES
    scale2 = 1.0 / (math.sqrt(width) * EPS) / LN2
    me_s = lax.axis_index("src")
    me_t = lax.axis_index("tgt")
    me_x, me_z = me_t // NZ, lax.rem(me_t, NZ)
    peers_s = [(lax.rem(me_s + k, NSRC), me_t) for k in (4, 3, 5, 2, 6, 1, 7)]
    peers_z = [(me_s, me_x * NZ + lax.rem(me_z + k, NZ)) for k in (4, 3, 5, 2, 6, 1, 7)]
    peers_x = [(me_s, lax.rem(me_x + k, NX) * NZ + me_z) for k in (2, 1, 3)]

    me_p = me_s * NX + me_x
    peers_p = [
        (lax.rem(me_s + b, NSRC), lax.rem(me_x + a, NX) * NZ + me_z)
        for a in (2, 1, 3, 0)
        for b in (4, 3, 5, 2, 6, 1, 7, 0)
        if a or b
    ]

    barrier = pltpu.get_barrier_semaphore()
    everyone = peers_z + peers_p
    for peer in everyone:
        pl.semaphore_signal(barrier, inc=1, device_id=peer, device_id_type=MESH)

    pending = []

    def send(phase, buf, me, peers):
        for peer in peers:
            pltpu.make_async_remote_copy(
                src_ref=buf.at[me],
                dst_ref=buf.at[me],
                send_sem=send_sem.at[phase],
                recv_sem=recv_sem.at[phase],
                device_id=peer,
                device_id_type=MESH,
            ).start()
        others = buf.at[pl.ds(0, len(peers))]
        done = pltpu.make_async_remote_copy(
            src_ref=others,
            dst_ref=others,
            send_sem=send_sem.at[phase],
            recv_sem=recv_sem.at[phase],
            device_id=peers[0],
            device_id_type=MESH,
        )
        pending.append(done)
        return done

    lane = lax.broadcasted_iota(jnp.int32, (L, L), 1)
    zero_tile = jnp.zeros((L, L), F32)

    def chunk(k):
        return pl.ds(k * L, L)

    loads[0].wait()
    loads[1].wait()
    rot[...] = dot_nn(source_ref[...], map_ref[...].astype(BF16)).astype(BF16)
    loads[2].wait()
    loads[3].wait()
    warm2 = warm_ref[...] * (1.0 / LN2)
    wide = 256

    def scores(half):
        for k in range(cols // wide):
            part = target_ref[pl.ds(k * wide, wide), :]
            warm_part = warm2[:, k * wide : (k + 1) * wide]

            def score_block(a, carry):
                block = rot[pl.ds(pl.multiple_of(a * 512, 512), 512), :]
                e_f32[pl.ds(a * 4, 4), :, pl.ds(k * wide, wide)] = (
                    dot_nt(block, part) * scale2 + warm_part
                ).reshape(4, L, wide)
                return carry

            first_block = half * hb * L // 512
            last_block = (half + 1) * hb * L // 512
            lax.fori_loop(first_block, last_block, score_block, 0, unroll=True)

    def first_row(a, acc):
        peak = e_f32[a, :, chunk(0)]
        for k in range(1, nk):
            peak = jnp.maximum(peak, e_f32[a, :, chunk(k)])
        peak = jnp.max(peak, axis=1, keepdims=True)
        total = jnp.exp2(e_f32[a, :, chunk(0)] - peak)
        for k in range(1, nk):
            total = total + jnp.exp2(e_f32[a, :, chunk(k)] - peak)
        total = jnp.sum(total, axis=1, keepdims=True)
        return jnp.where(lane == a, peak + jnp.log2(total), acc)

    def row_send(index, half, tile):
        row_z[index, half, me_z] = tile.T[half * hb : (half + 1) * hb]
        phase = 2 * (index * HALVES + half)
        return send(phase, row_z.at[index, half], me_z, peers_z)

    def row_receive(index, done, combine, consume):
        later = []
        for half in range(HALVES):
            done[half].wait_recv()
            row_x[index, half, me_x] = combine([row_z[index, half, i] for i in range(NZ)])
            phase = 2 * (index * HALVES + half) + 1
            later.append(send(phase, row_x.at[index, half], me_x, peers_x))
        for half in range(HALVES):
            later[half].wait_recv()
            consume(half, combine([row_x[index, half, i] for i in range(NX)]))

    sent = []
    for half in range(HALVES):
        scores(half)
        tile = lax.fori_loop(half * hb, (half + 1) * hb, first_row, zero_tile, unroll=4)
        if half == 0:
            pl.semaphore_wait(barrier, len(everyone))
        sent.append(row_send(0, half, tile))

    def col_reduce(index, combine, meanwhile=None):
        done = send(ROW_PHASES + index, col_s.at[index], me_s, peers_s)
        if meanwhile is not None:
            meanwhile()
        done.wait_recv()
        return combine([col_s[index, i] for i in range(NSRC)])

    def spread(half, value):
        u_t[half] = jnp.concatenate([value, jnp.zeros((L - hb, L), F32)], axis=0).T

    def column_of(half, a):
        return jnp.sum(
            jnp.where(lane == a - half * hb, u_t[half], 0.0), axis=1, keepdims=True
        )

    def fold(tile, op):
        parts = [tile[8 * i : 8 * i + 8] for i in range(L // 8)]
        while len(parts) > 1:
            parts = [op(parts[i], parts[i + 1]) for i in range(0, len(parts), 2)]
        return parts[0]

    def transposes():
        def one_source(a, carry):
            block = source_ref[pl.ds(pl.multiple_of(a * L, L), L), :].astype(F32)
            src_t[a] = block.T
            return carry

        lax.fori_loop(0, nb, one_source, 0)

        def one_target(a, carry):
            block = target_ref[pl.ds(pl.multiple_of(a * L, L), L), :].astype(F32)
            tgt_t[a] = block.T
            return carry

        lax.fori_loop(0, nk, one_target, 0)

    transposes()
    f_first = [None] * HALVES
    peaks = tuple(jnp.full((8, L), -jnp.inf, F32) for _ in range(nk))

    def first_cols(half, row_lse):
        nonlocal peaks
        f_first[half] = -math.log2(rows_all) - row_lse
        spread(half, f_first[half])

        def body(a, accs):
            f_col = column_of(half, a)
            return tuple(
                jnp.maximum(accs[k], fold(e_f32[a, :, chunk(k)] + f_col, jnp.maximum))
                for k in range(nk)
            )

        peaks = lax.fori_loop(half * hb, (half + 1) * hb, body, peaks, unroll=8)

    row_receive(0, sent, lse2, first_cols)
    peaks = [jnp.max(p, axis=0, keepdims=True) for p in peaks]

    def first_col_sum(half, a, accs):
        f_col = column_of(half, a)
        out = []
        for k in range(nk):
            e_val = jnp.exp2((e_f32[a, :, chunk(k)] + f_col) - peaks[k])
            e_f32[a, :, chunk(k)] = e_val
            out.append(accs[k] + fold(e_val, jnp.add))
        return tuple(out)

    zeros = tuple(jnp.zeros((8, L), F32) for _ in range(nk))
    sums = zeros
    for half in range(HALVES):
        sums = lax.fori_loop(
            half * hb,
            (half + 1) * hb,
            functools.partial(first_col_sum, half),
            sums,
            unroll=4,
        )
    for k in range(nk):
        total = jnp.sum(sums[k], axis=0, keepdims=True)
        col_s[0, me_s, :, chunk(k)] = peaks[k] + jnp.log2(total)

    def narrow():
        def body(a, carry):
            for k in range(nk):
                e_b16[a, :, chunk(k)] = e_f32[a, :, chunk(k)].astype(BF16)
            return carry

        lax.fori_loop(0, nb, body, 0)

    col_lse = col_reduce(0, lse2, narrow)
    g_first = warm2 - math.log2(cols_all) - col_lse
    local_weight = jnp.concatenate(
        [
            jnp.exp2(peaks[k] - col_lse[:, k * L : (k + 1) * L] - math.log2(cols_all))
            for k in range(nk)
        ],
        axis=1,
    )

    def row_pass(index, weight):
        weights = [weight[:, k * L : (k + 1) * L] for k in range(nk)]

        def body(a, acc):
            total = e_f32[a, :, chunk(0)] * weights[0]
            for k in range(1, nk):
                total = total + e_f32[a, :, chunk(k)] * weights[k]
            total = jnp.sum(total, axis=1, keepdims=True)
            return jnp.where(lane == a, total, acc)

        sent = []
        for half in range(HALVES):
            tile = lax.fori_loop(half * hb, (half + 1) * hb, body, zero_tile, unroll=hb)
            sent.append(row_send(index, half, tile))
        return sent

    def col_pass(index, sent):
        sums = zeros

        def consume(half, mass):
            nonlocal sums
            spread(half, 1.0 / (mass * rows_all))

            def body(a, accs):
                u_col = column_of(half, a)
                return tuple(
                    accs[k] + fold(e_f32[a, :, chunk(k)] * u_col, jnp.add) for k in range(nk)
                )

            sums = lax.fori_loop(half * hb, (half + 1) * hb, body, sums, unroll=hb)

        row_receive(index, sent, total_of, consume)
        for k in range(nk):
            total = jnp.sum(sums[k], axis=0, keepdims=True)
            col_s[index, me_s, :, chunk(k)] = total * local_weight[:, k * L : (k + 1) * L]

    weight = local_weight
    v_val = None
    for index in range(1, ROUNDS):
        col_pass(index, row_pass(index, weight))
        v_val = 1.0 / (col_reduce(index, total_of) * cols_all)
        weight = local_weight * v_val

    def barycentric():
        col_out[...] = (EPS * LN2) * (g_first + jnp.log2(v_val))
        pieces = [split(tgt_t[k] * weight[:, k * L : (k + 1) * L]) for k in range(nk)]
        both = jnp.concatenate(
            [
                jnp.concatenate([p[0] for p in pieces], axis=1),
                jnp.concatenate([p[1] for p in pieces], axis=1),
            ],
            axis=0,
        )

        def body(a, carry):
            block = e_b16[pl.ds(a * 4, 4)].reshape(4 * L, cols)
            out = dot_nt(block, both)
            high, low = split(out[:, :width] + out[:, width:])
            start = pl.multiple_of(a * 4 * L, 4 * L)
            bary[pl.ds(start, 4 * L), pl.ds(0, width)] = high
            bary[pl.ds(start, 4 * L), pl.ds(width, width)] = low
            return carry

        lax.fori_loop(0, nb // 4, body, 0, unroll=2)

    sent = row_pass(ROUNDS, weight)
    barycentric()
    inverse = []

    def last_rows(half, mass):
        row_out[pl.ds(half * hb, hb), :] = (EPS * LN2) * (
            f_first[half] - math.log2(rows_all) - jnp.log2(mass)
        )
        recip = 1.0 / mass
        inverse.extend(recip[i : i + 1, :] for i in range(hb))

    row_receive(ROUNDS, sent, total_of, last_rows)
    pieces = [split(src_t[a] * inverse[a]) for a in range(nb)]
    stacked = jnp.concatenate(
        [
            jnp.concatenate([p[0] for p in pieces], axis=1),
            jnp.concatenate([p[1] for p in pieces], axis=1),
        ],
        axis=0,
    )
    out = dot_nn(stacked, bary[...])
    cross[...] = (
        out[:width, :width] + out[:width, width:] + out[width:, :width] + out[width:, width:]
    ).reshape(NPART, width // NPART, width)

    phase = ROW_PHASES + ROUNDS
    cross_p[me_p] = cross[me_p]
    for peer in peers_p:
        pltpu.make_async_remote_copy(
            src_ref=cross.at[peer[0] * NX + peer[1] // NZ],
            dst_ref=cross_p.at[me_p],
            send_sem=send_sem.at[phase],
            recv_sem=recv_sem.at[phase],
            device_id=peer,
            device_id_type=MESH,
        ).start()
    others = cross_p.at[pl.ds(0, len(peers_p))]
    done = pltpu.make_async_remote_copy(
        src_ref=others,
        dst_ref=others,
        send_sem=send_sem.at[phase],
        recv_sem=recv_sem.at[phase],
        device_id=peers_p[0],
        device_id_type=MESH,
    )
    pending.append(done)
    done.wait_recv()
    cross_z[me_z] = jnp.sum(cross_p[...], axis=0)
    send(phase + 1, cross_z, me_z, peers_z).wait_recv()
    cross_g[me_p] = jnp.sum(cross_z[...], axis=0)
    send(phase + 2, cross_g, me_p, peers_p).wait_recv()

    for done in pending:
        done.wait_send()


def polar_kernel(cross_ref, row_ref, col_ref, row_out, col_out, map_out, result, sems):
    stores = [
        pltpu.make_async_copy(row_ref, row_out, sems.at[0]),
        pltpu.make_async_copy(col_ref, col_out, sems.at[1]),
        pltpu.make_async_copy(result, map_out, sems.at[2]),
    ]
    stores[0].start()
    stores[1].start()
    width = result.shape[0]
    matrix = cross_ref[...].reshape(width, width)
    norm = jnp.sum(jnp.sum(matrix * matrix, axis=1, keepdims=True), axis=0, keepdims=True)
    iterate = matrix / jnp.sqrt(norm + 1e-06)

    def newton(_, iterate):
        high, low = split(iterate)
        pair = jnp.concatenate([high, low], axis=1)
        twice = jnp.concatenate(
            [jnp.concatenate([high, high], axis=1), jnp.concatenate([low, low], axis=1)], axis=0
        )
        gram = dot_nt(pair, twice)
        gram = gram[:, :width] + gram[:, width:]
        pair_g = jnp.concatenate(split(gram), axis=1)
        stack = jnp.concatenate([pair, pair], axis=0)
        prod = dot_nn(pair_g, stack)
        return 1.5 * iterate - 0.5 * (prod[:, :width] + prod[:, width:])

    result[...] = lax.fori_loop(0, NEWTON, newton, iterate, unroll=10)
    stores[2].start()
    for store in stores:
        store.wait()


def shards(source, target, start_map, warm_potential):
    rows, width = source.shape
    cols = target.shape[0]
    rows_all, cols_all = rows * lax.axis_size("src"), cols * lax.axis_size("tgt")
    nb, nk = rows // L, cols // L
    phases = ROW_PHASES + ROUNDS + 3
    vmem = pltpu.VMEM
    pots = (jax.ShapeDtypeStruct((nb, L), F32), jax.ShapeDtypeStruct((1, cols), F32))
    part_shape = (NPART, width // NPART, width)
    row_pot, col_pot, cross = pl.pallas_call(
        functools.partial(kernel, rows_all, cols_all),
        out_shape=(*pots, jax.ShapeDtypeStruct(part_shape, F32)),
        in_specs=[pl.BlockSpec(memory_space=pltpu.HBM)] * 4,
        out_specs=[pl.BlockSpec(memory_space=vmem)] * 3,
        scratch_shapes=[
            vmem((rows, width), BF16),
            vmem((cols, width), BF16),
            vmem((width, width), F32),
            vmem((1, cols), F32),
            vmem((rows, width), BF16),
            vmem((nb, L, cols), F32),
            vmem((nb, L, cols), BF16),
            vmem((nb, width, L), F32),
            vmem((nk, width, L), F32),
            vmem((rows, 2 * width), BF16),
            vmem((HALVES, L, L), F32),
            vmem(part_shape, F32),
            vmem((ROUNDS + 1, HALVES, NZ, nb // HALVES, L), F32),
            vmem((ROUNDS + 1, HALVES, NX, nb // HALVES, L), F32),
            vmem((ROUNDS, NSRC, 1, cols), F32),
            vmem(part_shape, F32),
            vmem((NZ, *part_shape[1:]), F32),
            pltpu.SemaphoreType.DMA((phases,)),
            pltpu.SemaphoreType.DMA((phases,)),
            pltpu.SemaphoreType.DMA((4,)),
        ],
        compiler_params=pltpu.CompilerParams(
            collective_id=0, has_side_effects=True, vmem_limit_bytes=40 << 20
        ),
        name="sinkhorn",
    )(
        *(
            pltpu.with_memory_space_constraint(arg, pltpu.HBM)
            for arg in (source, target, start_map, warm_potential.reshape(1, cols))
        )
    )
    row_pot, col_pot, new_map = pl.pallas_call(
        polar_kernel,
        out_shape=(*pots, jax.ShapeDtypeStruct((width, width), F32)),
        in_specs=[pl.BlockSpec(memory_space=vmem)] * 3,
        out_specs=[pl.BlockSpec(memory_space=pltpu.HBM)] * 3,
        scratch_shapes=[vmem((width, width), F32), pltpu.SemaphoreType.DMA((3,))],
        compiler_params=pltpu.CompilerParams(vmem_limit_bytes=8 << 20),
        name="polar",
    )(cross, row_pot, col_pot)
    return row_pot.reshape(rows), col_pot.reshape(cols), new_map


def solution(mesh):
    placed = (P("src", None), P("tgt", None), P(), P("tgt"))
    return jax.shard_map(
        shards,
        mesh=mesh,
        in_specs=placed,
        out_specs=(P("src"), P("tgt"), P()),
        check_vma=False,
    )
```

```python
import functools
import math

import jax
import jax.numpy as jnp
from jax import lax
from jax.experimental import pallas as pl
from jax.experimental.pallas import tpu as pltpu
from jax.sharding import PartitionSpec as P

ROUNDS = 3
NEWTON = 10
EPS = 0.05
LN2 = math.log(2.0)
MESH = pl.DeviceIdType.MESH
F32 = jnp.float32
BF16 = jnp.bfloat16
NX, NY, NZ, NC = 4, 4, 8, 2
NSRC = NY * NC
NPART = NSRC * NX
HALVES = 2
ROW_PHASES = 2 * HALVES * (ROUNDS + 1)
L = 128


def split(value):
    high = value.astype(BF16)
    low = (value - high.astype(F32)).astype(BF16)
    return high, low


def dot_nt(a, b):
    return lax.dot_general(a, b, (((1,), (1,)), ((), ())), preferred_element_type=F32)


def dot_nn(a, b):
    return jnp.dot(a, b, preferred_element_type=F32)


def lse2(parts):
    peak = parts[0]
    for part in parts[1:]:
        peak = jnp.maximum(peak, part)
    total = jnp.exp2(parts[0] - peak)
    for part in parts[1:]:
        total = total + jnp.exp2(part - peak)
    return peak + jnp.log2(total)


def total_of(parts):
    total = parts[0]
    for part in parts[1:]:
        total = total + part
    return total


def kernel(
    rows_all,
    cols_all,
    source_hbm,
    target_hbm,
    map_hbm,
    warm_hbm,
    row_out,
    col_out,
    cross_g,
    source_ref,
    target_ref,
    map_ref,
    warm_ref,
    rot,
    e_f32,
    e_b16,
    src_t,
    tgt_t,
    bary,
    u_t,
    cross,
    row_z,
    row_x,
    col_s,
    cross_p,
    cross_z,
    send_sem,
    recv_sem,
    load_sem,
):
    loads = [
        pltpu.make_async_copy(hbm, ref, load_sem.at[i])
        for i, (hbm, ref) in enumerate(
            [
                (map_hbm, map_ref),
                (source_hbm, source_ref),
                (target_hbm, target_ref),
                (warm_hbm, warm_ref),
            ]
        )
    ]
    for load in loads:
        load.start()
    rows, width = source_ref.shape
    cols = target_ref.shape[0]
    nb, nk = rows // L, cols // L
    hb = nb // HALVES
    scale2 = 1.0 / (math.sqrt(width) * EPS) / LN2
    me_s = lax.axis_index("src")
    me_t = lax.axis_index("tgt")
    me_x, me_z = me_t // NZ, lax.rem(me_t, NZ)
    peers_s = [(lax.rem(me_s + k, NSRC), me_t) for k in (4, 3, 5, 2, 6, 1, 7)]
    peers_z = [(me_s, me_x * NZ + lax.rem(me_z + k, NZ)) for k in (4, 3, 5, 2, 6, 1, 7)]
    peers_x = [(me_s, lax.rem(me_x + k, NX) * NZ + me_z) for k in (2, 1, 3)]

    me_p = me_s * NX + me_x
    peers_p = [
        (lax.rem(me_s + b, NSRC), lax.rem(me_x + a, NX) * NZ + me_z)
        for a in (2, 1, 3, 0)
        for b in (4, 3, 5, 2, 6, 1, 7, 0)
        if a or b
    ]

    barrier = pltpu.get_barrier_semaphore()
    everyone = peers_z + peers_s + peers_x
    for peer in everyone:
        pl.semaphore_signal(barrier, inc=1, device_id=peer, device_id_type=MESH)

    pending = []

    def send(phase, buf, me, peers):
        for peer in peers:
            pltpu.make_async_remote_copy(
                src_ref=buf.at[me],
                dst_ref=buf.at[me],
                send_sem=send_sem.at[phase],
                recv_sem=recv_sem.at[phase],
                device_id=peer,
                device_id_type=MESH,
            ).start()
        others = buf.at[pl.ds(0, len(peers))]
        done = pltpu.make_async_remote_copy(
            src_ref=others,
            dst_ref=others,
            send_sem=send_sem.at[phase],
            recv_sem=recv_sem.at[phase],
            device_id=peers[0],
            device_id_type=MESH,
        )
        pending.append(done)
        return done

    lane = lax.broadcasted_iota(jnp.int32, (L, L), 1)
    zero_tile = jnp.zeros((L, L), F32)

    def chunk(k):
        return pl.ds(k * L, L)

    loads[0].wait()
    loads[1].wait()
    rot[...] = dot_nn(source_ref[...], map_ref[...].astype(BF16)).astype(BF16)
    loads[2].wait()
    loads[3].wait()
    warm2 = warm_ref[...] * (1.0 / LN2)
    wide = 256

    def scores(half):
        for k in range(cols // wide):
            part = target_ref[pl.ds(k * wide, wide), :]
            warm_part = warm2[:, k * wide : (k + 1) * wide]

            def score_block(a, carry):
                block = rot[pl.ds(pl.multiple_of(a * 512, 512), 512), :]
                e_f32[pl.ds(a * 4, 4), :, pl.ds(k * wide, wide)] = (
                    dot_nt(block, part) * scale2 + warm_part
                ).reshape(4, L, wide)
                return carry

            first_block = half * hb * L // 512
            last_block = (half + 1) * hb * L // 512
            lax.fori_loop(first_block, last_block, score_block, 0, unroll=True)

    def first_row(a, acc):
        peak = e_f32[a, :, chunk(0)]
        for k in range(1, nk):
            peak = jnp.maximum(peak, e_f32[a, :, chunk(k)])
        peak = jnp.max(peak, axis=1, keepdims=True)
        total = jnp.exp2(e_f32[a, :, chunk(0)] - peak)
        for k in range(1, nk):
            total = total + jnp.exp2(e_f32[a, :, chunk(k)] - peak)
        total = jnp.sum(total, axis=1, keepdims=True)
        return jnp.where(lane == a, peak + jnp.log2(total), acc)

    def row_send(index, half, tile):
        row_z[index, half, me_z] = tile.T[half * hb : (half + 1) * hb]
        phase = 2 * (index * HALVES + half)
        return send(phase, row_z.at[index, half], me_z, peers_z)

    def row_receive(index, done, combine, consume):
        later = []
        for half in range(HALVES):
            done[half].wait_recv()
            row_x[index, half, me_x] = combine([row_z[index, half, i] for i in range(NZ)])
            phase = 2 * (index * HALVES + half) + 1
            later.append(send(phase, row_x.at[index, half], me_x, peers_x))
        for half in range(HALVES):
            later[half].wait_recv()
            consume(half, combine([row_x[index, half, i] for i in range(NX)]))

    sent = []
    for half in range(HALVES):
        scores(half)
        tile = lax.fori_loop(half * hb, (half + 1) * hb, first_row, zero_tile, unroll=4)
        if half == 0:
            pl.semaphore_wait(barrier, len(everyone))
        sent.append(row_send(0, half, tile))

    def col_reduce(index, combine, meanwhile=None):
        done = send(ROW_PHASES + index, col_s.at[index], me_s, peers_s)
        if meanwhile is not None:
            meanwhile()
        done.wait_recv()
        return combine([col_s[index, i] for i in range(NSRC)])

    def spread(half, value):
        u_t[half] = jnp.concatenate([value, jnp.zeros((L - hb, L), F32)], axis=0).T

    def column_of(half, a):
        return jnp.sum(
            jnp.where(lane == a - half * hb, u_t[half], 0.0), axis=1, keepdims=True
        )

    def fold(tile, op):
        parts = [tile[8 * i : 8 * i + 8] for i in range(L // 8)]
        while len(parts) > 1:
            parts = [op(parts[i], parts[i + 1]) for i in range(0, len(parts), 2)]
        return parts[0]

    def transposes():
        def one_source(a, carry):
            block = source_ref[pl.ds(pl.multiple_of(a * L, L), L), :].astype(F32)
            src_t[a] = block.T
            return carry

        lax.fori_loop(0, nb, one_source, 0)

        def one_target(a, carry):
            block = target_ref[pl.ds(pl.multiple_of(a * L, L), L), :].astype(F32)
            tgt_t[a] = block.T
            return carry

        lax.fori_loop(0, nk, one_target, 0)

    transposes()
    f_first = [None] * HALVES
    peaks = tuple(jnp.full((8, L), -jnp.inf, F32) for _ in range(nk))

    def first_cols(half, row_lse):
        nonlocal peaks
        f_first[half] = -math.log2(rows_all) - row_lse
        spread(half, f_first[half])

        def body(a, accs):
            f_col = column_of(half, a)
            return tuple(
                jnp.maximum(accs[k], fold(e_f32[a, :, chunk(k)] + f_col, jnp.maximum))
                for k in range(nk)
            )

        peaks = lax.fori_loop(half * hb, (half + 1) * hb, body, peaks, unroll=8)

    row_receive(0, sent, lse2, first_cols)
    peaks = [jnp.max(p, axis=0, keepdims=True) for p in peaks]

    def first_col_sum(half, a, accs):
        f_col = column_of(half, a)
        out = []
        for k in range(nk):
            e_val = jnp.exp2((e_f32[a, :, chunk(k)] + f_col) - peaks[k])
            e_f32[a, :, chunk(k)] = e_val
            out.append(accs[k] + fold(e_val, jnp.add))
        return tuple(out)

    zeros = tuple(jnp.zeros((8, L), F32) for _ in range(nk))
    sums = zeros
    for half in range(HALVES):
        sums = lax.fori_loop(
            half * hb,
            (half + 1) * hb,
            functools.partial(first_col_sum, half),
            sums,
            unroll=4,
        )
    for k in range(nk):
        total = jnp.sum(sums[k], axis=0, keepdims=True)
        col_s[0, me_s, :, chunk(k)] = peaks[k] + jnp.log2(total)

    def narrow():
        def body(a, carry):
            for k in range(nk):
                e_b16[a, :, chunk(k)] = e_f32[a, :, chunk(k)].astype(BF16)
            return carry

        lax.fori_loop(0, nb, body, 0)

    col_lse = col_reduce(0, lse2, narrow)
    g_first = warm2 - math.log2(cols_all) - col_lse
    local_weight = jnp.concatenate(
        [
            jnp.exp2(peaks[k] - col_lse[:, k * L : (k + 1) * L] - math.log2(cols_all))
            for k in range(nk)
        ],
        axis=1,
    )

    def row_pass(index, weight):
        weights = [weight[:, k * L : (k + 1) * L] for k in range(nk)]

        def body(a, acc):
            total = e_f32[a, :, chunk(0)] * weights[0]
            for k in range(1, nk):
                total = total + e_f32[a, :, chunk(k)] * weights[k]
            total = jnp.sum(total, axis=1, keepdims=True)
            return jnp.where(lane == a, total, acc)

        sent = []
        for half in range(HALVES):
            tile = lax.fori_loop(half * hb, (half + 1) * hb, body, zero_tile, unroll=hb)
            sent.append(row_send(index, half, tile))
        return sent

    def col_pass(index, sent):
        sums = zeros

        def consume(half, mass):
            nonlocal sums
            spread(half, 1.0 / (mass * rows_all))

            def body(a, accs):
                u_col = column_of(half, a)
                return tuple(
                    accs[k] + fold(e_f32[a, :, chunk(k)] * u_col, jnp.add) for k in range(nk)
                )

            sums = lax.fori_loop(half * hb, (half + 1) * hb, body, sums, unroll=hb)

        row_receive(index, sent, total_of, consume)
        for k in range(nk):
            total = jnp.sum(sums[k], axis=0, keepdims=True)
            col_s[index, me_s, :, chunk(k)] = total * local_weight[:, k * L : (k + 1) * L]

    weight = local_weight
    v_val = None
    for index in range(1, ROUNDS):
        col_pass(index, row_pass(index, weight))
        v_val = 1.0 / (col_reduce(index, total_of) * cols_all)
        weight = local_weight * v_val

    def barycentric():
        col_out[...] = (EPS * LN2) * (g_first + jnp.log2(v_val))
        pieces = [split(tgt_t[k] * weight[:, k * L : (k + 1) * L]) for k in range(nk)]
        both = jnp.concatenate(
            [
                jnp.concatenate([p[0] for p in pieces], axis=1),
                jnp.concatenate([p[1] for p in pieces], axis=1),
            ],
            axis=0,
        )

        def body(a, carry):
            block = e_b16[pl.ds(a * 4, 4)].reshape(4 * L, cols)
            out = dot_nt(block, both)
            high, low = split(out[:, :width] + out[:, width:])
            start = pl.multiple_of(a * 4 * L, 4 * L)
            bary[pl.ds(start, 4 * L), pl.ds(0, width)] = high
            bary[pl.ds(start, 4 * L), pl.ds(width, width)] = low
            return carry

        lax.fori_loop(0, nb // 4, body, 0, unroll=2)

    sent = row_pass(ROUNDS, weight)
    barycentric()
    inverse = []

    def last_rows(half, mass):
        row_out[pl.ds(half * hb, hb), :] = (EPS * LN2) * (
            f_first[half] - math.log2(rows_all) - jnp.log2(mass)
        )
        recip = 1.0 / mass
        inverse.extend(recip[i : i + 1, :] for i in range(hb))

    row_receive(ROUNDS, sent, total_of, last_rows)
    pieces = [split(src_t[a] * inverse[a]) for a in range(nb)]
    stacked = jnp.concatenate(
        [
            jnp.concatenate([p[0] for p in pieces], axis=1),
            jnp.concatenate([p[1] for p in pieces], axis=1),
        ],
        axis=0,
    )
    out = dot_nn(stacked, bary[...])
    cross[...] = (
        out[:width, :width] + out[:width, width:] + out[width:, :width] + out[width:, width:]
    ).reshape(NPART, width // NPART, width)

    phase = ROW_PHASES + ROUNDS
    cross_p[me_p] = cross[me_p]
    for peer in peers_p:
        pltpu.make_async_remote_copy(
            src_ref=cross.at[peer[0] * NX + peer[1] // NZ],
            dst_ref=cross_p.at[me_p],
            send_sem=send_sem.at[phase],
            recv_sem=recv_sem.at[phase],
            device_id=peer,
            device_id_type=MESH,
        ).start()
    others = cross_p.at[pl.ds(0, len(peers_p))]
    done = pltpu.make_async_remote_copy(
        src_ref=others,
        dst_ref=others,
        send_sem=send_sem.at[phase],
        recv_sem=recv_sem.at[phase],
        device_id=peers_p[0],
        device_id_type=MESH,
    )
    pending.append(done)
    done.wait_recv()
    cross_z[me_z] = jnp.sum(cross_p[...], axis=0)
    send(phase + 1, cross_z, me_z, peers_z).wait_recv()
    cross_g[me_p] = jnp.sum(cross_z[...], axis=0)
    send(phase + 2, cross_g, me_p, peers_p).wait_recv()

    for done in pending:
        done.wait_send()


def polar_kernel(cross_ref, row_ref, col_ref, row_out, col_out, map_out, result, sems):
    stores = [
        pltpu.make_async_copy(row_ref, row_out, sems.at[0]),
        pltpu.make_async_copy(col_ref, col_out, sems.at[1]),
        pltpu.make_async_copy(result, map_out, sems.at[2]),
    ]
    stores[0].start()
    stores[1].start()
    width = result.shape[0]
    matrix = cross_ref[...].reshape(width, width)
    norm = jnp.sum(jnp.sum(matrix * matrix, axis=1, keepdims=True), axis=0, keepdims=True)
    iterate = matrix / jnp.sqrt(norm + 1e-06)

    def newton(_, iterate):
        high, low = split(iterate)
        pair = jnp.concatenate([high, low], axis=1)
        twice = jnp.concatenate(
            [jnp.concatenate([high, high], axis=1), jnp.concatenate([low, low], axis=1)], axis=0
        )
        gram = dot_nt(pair, twice)
        gram = gram[:, :width] + gram[:, width:]
        pair_g = jnp.concatenate(split(gram), axis=1)
        stack = jnp.concatenate([pair, pair], axis=0)
        prod = dot_nn(pair_g, stack)
        return 1.5 * iterate - 0.5 * (prod[:, :width] + prod[:, width:])

    result[...] = lax.fori_loop(0, NEWTON, newton, iterate, unroll=10)
    stores[2].start()
    for store in stores:
        store.wait()


def shards(source, target, start_map, warm_potential):
    rows, width = source.shape
    cols = target.shape[0]
    rows_all, cols_all = rows * lax.axis_size("src"), cols * lax.axis_size("tgt")
    nb, nk = rows // L, cols // L
    phases = ROW_PHASES + ROUNDS + 3
    vmem = pltpu.VMEM
    pots = (jax.ShapeDtypeStruct((nb, L), F32), jax.ShapeDtypeStruct((1, cols), F32))
    part_shape = (NPART, width // NPART, width)
    row_pot, col_pot, cross = pl.pallas_call(
        functools.partial(kernel, rows_all, cols_all),
        out_shape=(*pots, jax.ShapeDtypeStruct(part_shape, F32)),
        in_specs=[pl.BlockSpec(memory_space=pltpu.HBM)] * 4,
        out_specs=[pl.BlockSpec(memory_space=vmem)] * 3,
        scratch_shapes=[
            vmem((rows, width), BF16),
            vmem((cols, width), BF16),
            vmem((width, width), F32),
            vmem((1, cols), F32),
            vmem((rows, width), BF16),
            vmem((nb, L, cols), F32),
            vmem((nb, L, cols), BF16),
            vmem((nb, width, L), F32),
            vmem((nk, width, L), F32),
            vmem((rows, 2 * width), BF16),
            vmem((HALVES, L, L), F32),
            vmem(part_shape, F32),
            vmem((ROUNDS + 1, HALVES, NZ, nb // HALVES, L), F32),
            vmem((ROUNDS + 1, HALVES, NX, nb // HALVES, L), F32),
            vmem((ROUNDS, NSRC, 1, cols), F32),
            vmem(part_shape, F32),
            vmem((NZ, *part_shape[1:]), F32),
            pltpu.SemaphoreType.DMA((phases,)),
            pltpu.SemaphoreType.DMA((phases,)),
            pltpu.SemaphoreType.DMA((4,)),
        ],
        compiler_params=pltpu.CompilerParams(
            collective_id=0, has_side_effects=True, vmem_limit_bytes=40 << 20
        ),
        name="sinkhorn",
    )(
        *(
            pltpu.with_memory_space_constraint(arg, pltpu.HBM)
            for arg in (source, target, start_map, warm_potential.reshape(1, cols))
        )
    )
    row_pot, col_pot, new_map = pl.pallas_call(
        polar_kernel,
        out_shape=(*pots, jax.ShapeDtypeStruct((width, width), F32)),
        in_specs=[pl.BlockSpec(memory_space=vmem)] * 3,
        out_specs=[pl.BlockSpec(memory_space=pltpu.HBM)] * 3,
        scratch_shapes=[vmem((width, width), F32), pltpu.SemaphoreType.DMA((3,))],
        compiler_params=pltpu.CompilerParams(vmem_limit_bytes=8 << 20),
        name="polar",
    )(cross, row_pot, col_pot)
    return row_pot.reshape(rows), col_pot.reshape(cols), new_map


def solution(mesh):
    placed = (P("src", None), P("tgt", None), P(), P("tgt"))
    return jax.shard_map(
        shards,
        mesh=mesh,
        in_specs=placed,
        out_specs=(P("src"), P("tgt"), P()),
        check_vma=False,
    )
```

```python
import functools
import math

import jax
import jax.numpy as jnp
from jax import lax
from jax.experimental import pallas as pl
from jax.experimental.pallas import tpu as pltpu
from jax.sharding import PartitionSpec as P

ROUNDS = 3
NEWTON = 10
EPS = 0.05
LN2 = math.log(2.0)
MESH = pl.DeviceIdType.MESH
F32 = jnp.float32
BF16 = jnp.bfloat16
NX, NY, NZ, NC = 4, 4, 8, 2
NSRC = NY * NC
NPART = NSRC * NX
HALVES = 2
ROW_PHASES = 2 * HALVES * (ROUNDS + 1)
L = 128


def split(value):
    high = value.astype(BF16)
    low = (value - high.astype(F32)).astype(BF16)
    return high, low


def dot_nt(a, b):
    return lax.dot_general(a, b, (((1,), (1,)), ((), ())), preferred_element_type=F32)


def dot_nn(a, b):
    return jnp.dot(a, b, preferred_element_type=F32)


def lse2(parts):
    peak = parts[0]
    for part in parts[1:]:
        peak = jnp.maximum(peak, part)
    total = jnp.exp2(parts[0] - peak)
    for part in parts[1:]:
        total = total + jnp.exp2(part - peak)
    return peak + jnp.log2(total)


def total_of(parts):
    total = parts[0]
    for part in parts[1:]:
        total = total + part
    return total


def kernel(
    rows_all,
    cols_all,
    source_hbm,
    target_hbm,
    map_hbm,
    warm_hbm,
    row_out,
    col_out,
    cross_g,
    source_ref,
    target_ref,
    map_ref,
    warm_ref,
    rot,
    e_f32,
    e_b16,
    src_t,
    tgt_t,
    bary,
    u_t,
    cross,
    row_z,
    row_x,
    col_s,
    cross_p,
    cross_z,
    send_sem,
    recv_sem,
    load_sem,
):
    loads = [
        pltpu.make_async_copy(hbm, ref, load_sem.at[i])
        for i, (hbm, ref) in enumerate(
            [
                (map_hbm, map_ref),
                (source_hbm, source_ref),
                (target_hbm, target_ref),
                (warm_hbm, warm_ref),
            ]
        )
    ]
    for load in loads:
        load.start()
    rows, width = source_ref.shape
    cols = target_ref.shape[0]
    nb, nk = rows // L, cols // L
    hb = nb // HALVES
    scale2 = 1.0 / (math.sqrt(width) * EPS) / LN2
    me_s = lax.axis_index("src")
    me_t = lax.axis_index("tgt")
    me_x, me_z = me_t // NZ, lax.rem(me_t, NZ)
    peers_s = [(lax.rem(me_s + k, NSRC), me_t) for k in (4, 3, 5, 2, 6, 1, 7)]
    peers_z = [(me_s, me_x * NZ + lax.rem(me_z + k, NZ)) for k in (4, 3, 5, 2, 6, 1, 7)]
    peers_x = [(me_s, lax.rem(me_x + k, NX) * NZ + me_z) for k in (2, 1, 3)]

    me_p = me_s * NX + me_x
    peers_p = [
        (lax.rem(me_s + b, NSRC), lax.rem(me_x + a, NX) * NZ + me_z)
        for a in (2, 1, 3, 0)
        for b in (4, 3, 5, 2, 6, 1, 7, 0)
        if a or b
    ]

    barrier = pltpu.get_barrier_semaphore()
    everyone = peers_z + peers_s + peers_x
    for peer in everyone:
        pl.semaphore_signal(barrier, inc=1, device_id=peer, device_id_type=MESH)

    pending = []

    def send(phase, buf, me, peers):
        for peer in peers:
            pltpu.make_async_remote_copy(
                src_ref=buf.at[me],
                dst_ref=buf.at[me],
                send_sem=send_sem.at[phase],
                recv_sem=recv_sem.at[phase],
                device_id=peer,
                device_id_type=MESH,
            ).start()
        others = buf.at[pl.ds(0, len(peers))]
        done = pltpu.make_async_remote_copy(
            src_ref=others,
            dst_ref=others,
            send_sem=send_sem.at[phase],
            recv_sem=recv_sem.at[phase],
            device_id=peers[0],
            device_id_type=MESH,
        )
        pending.append(done)
        return done

    lane = lax.broadcasted_iota(jnp.int32, (L, L), 1)
    zero_tile = jnp.zeros((L, L), F32)

    def chunk(k):
        return pl.ds(k * L, L)

    loads[0].wait()
    loads[1].wait()
    rot[...] = dot_nn(source_ref[...], map_ref[...].astype(BF16)).astype(BF16)
    loads[2].wait()
    loads[3].wait()
    warm2 = warm_ref[...] * (1.0 / LN2)
    wide = 256

    def scores(half):
        for k in range(cols // wide):
            part = target_ref[pl.ds(k * wide, wide), :]
            warm_part = warm2[:, k * wide : (k + 1) * wide]

            def score_block(a, carry):
                block = rot[pl.ds(pl.multiple_of(a * 512, 512), 512), :]
                e_f32[pl.ds(a * 4, 4), :, pl.ds(k * wide, wide)] = (
                    dot_nt(block, part) * scale2 + warm_part
                ).reshape(4, L, wide)
                return carry

            first_block = half * hb * L // 512
            last_block = (half + 1) * hb * L // 512
            lax.fori_loop(first_block, last_block, score_block, 0, unroll=True)

    def first_row(a, acc):
        peak = e_f32[a, :, chunk(0)]
        for k in range(1, nk):
            peak = jnp.maximum(peak, e_f32[a, :, chunk(k)])
        peak = jnp.max(peak, axis=1, keepdims=True)
        total = jnp.exp2(e_f32[a, :, chunk(0)] - peak)
        for k in range(1, nk):
            total = total + jnp.exp2(e_f32[a, :, chunk(k)] - peak)
        total = jnp.sum(total, axis=1, keepdims=True)
        return jnp.where(lane == a, peak + jnp.log2(total), acc)

    def row_send(index, half, tile):
        row_z[index, half, me_z] = tile.T[half * hb : (half + 1) * hb]
        phase = 2 * (index * HALVES + half)
        return send(phase, row_z.at[index, half], me_z, peers_z)

    def row_receive(index, done, combine, consume):
        later = []
        for half in range(HALVES):
            done[half].wait_recv()
            row_x[index, half, me_x] = combine([row_z[index, half, i] for i in range(NZ)])
            phase = 2 * (index * HALVES + half) + 1
            later.append(send(phase, row_x.at[index, half], me_x, peers_x))
        for half in range(HALVES):
            later[half].wait_recv()
            consume(half, combine([row_x[index, half, i] for i in range(NX)]))

    sent = []
    for half in range(HALVES):
        scores(half)
        tile = lax.fori_loop(half * hb, (half + 1) * hb, first_row, zero_tile, unroll=4)
        if half == 0:
            pl.semaphore_wait(barrier, len(everyone))
        sent.append(row_send(0, half, tile))

    def col_reduce(index, combine, meanwhile=None):
        done = send(ROW_PHASES + index, col_s.at[index], me_s, peers_s)
        if meanwhile is not None:
            meanwhile()
        done.wait_recv()
        return combine([col_s[index, i] for i in range(NSRC)])

    def spread(half, value):
        u_t[half] = jnp.concatenate([value, jnp.zeros((L - hb, L), F32)], axis=0).T

    def column_of(half, a):
        return jnp.sum(
            jnp.where(lane == a - half * hb, u_t[half], 0.0), axis=1, keepdims=True
        )

    def fold(tile, op):
        parts = [tile[8 * i : 8 * i + 8] for i in range(L // 8)]
        while len(parts) > 1:
            parts = [op(parts[i], parts[i + 1]) for i in range(0, len(parts), 2)]
        return parts[0]

    def transposes():
        def one_source(a, carry):
            block = source_ref[pl.ds(pl.multiple_of(a * L, L), L), :].astype(F32)
            src_t[a] = block.T
            return carry

        lax.fori_loop(0, nb, one_source, 0)

        def one_target(a, carry):
            block = target_ref[pl.ds(pl.multiple_of(a * L, L), L), :].astype(F32)
            tgt_t[a] = block.T
            return carry

        lax.fori_loop(0, nk, one_target, 0)

    transposes()
    f_first = [None] * HALVES
    peaks = tuple(jnp.full((8, L), -jnp.inf, F32) for _ in range(nk))

    def first_cols(half, row_lse):
        nonlocal peaks
        f_first[half] = -math.log2(rows_all) - row_lse
        spread(half, f_first[half])

        def body(a, accs):
            f_col = column_of(half, a)
            return tuple(
                jnp.maximum(accs[k], fold(e_f32[a, :, chunk(k)] + f_col, jnp.maximum))
                for k in range(nk)
            )

        peaks = lax.fori_loop(half * hb, (half + 1) * hb, body, peaks, unroll=8)

    row_receive(0, sent, lse2, first_cols)
    peaks = [jnp.max(p, axis=0, keepdims=True) for p in peaks]

    def first_col_sum(half, a, accs):
        f_col = column_of(half, a)
        out = []
        for k in range(nk):
            e_val = jnp.exp2((e_f32[a, :, chunk(k)] + f_col) - peaks[k])
            e_f32[a, :, chunk(k)] = e_val
            out.append(accs[k] + fold(e_val, jnp.add))
        return tuple(out)

    zeros = tuple(jnp.zeros((8, L), F32) for _ in range(nk))
    sums = zeros
    for half in range(HALVES):
        sums = lax.fori_loop(
            half * hb,
            (half + 1) * hb,
            functools.partial(first_col_sum, half),
            sums,
            unroll=4,
        )
    for k in range(nk):
        total = jnp.sum(sums[k], axis=0, keepdims=True)
        col_s[0, me_s, :, chunk(k)] = peaks[k] + jnp.log2(total)

    def narrow():
        def body(a, carry):
            for k in range(nk):
                e_b16[a, :, chunk(k)] = e_f32[a, :, chunk(k)].astype(BF16)
            return carry

        lax.fori_loop(0, nb, body, 0)

    col_lse = col_reduce(0, lse2, narrow)
    g_first = warm2 - math.log2(cols_all) - col_lse
    local_weight = jnp.concatenate(
        [
            jnp.exp2(peaks[k] - col_lse[:, k * L : (k + 1) * L] - math.log2(cols_all))
            for k in range(nk)
        ],
        axis=1,
    )

    def row_pass(index, weight):
        weights = [weight[:, k * L : (k + 1) * L] for k in range(nk)]

        def body(a, acc):
            total = e_f32[a, :, chunk(0)] * weights[0]
            for k in range(1, nk):
                total = total + e_f32[a, :, chunk(k)] * weights[k]
            total = jnp.sum(total, axis=1, keepdims=True)
            return jnp.where(lane == a, total, acc)

        sent = []
        for half in range(HALVES):
            tile = lax.fori_loop(half * hb, (half + 1) * hb, body, zero_tile, unroll=hb)
            sent.append(row_send(index, half, tile))
        return sent

    def col_pass(index, sent):
        sums = zeros

        def consume(half, mass):
            nonlocal sums
            spread(half, 1.0 / (mass * rows_all))

            def body(a, accs):
                u_col = column_of(half, a)
                return tuple(
                    accs[k] + fold(e_f32[a, :, chunk(k)] * u_col, jnp.add) for k in range(nk)
                )

            sums = lax.fori_loop(half * hb, (half + 1) * hb, body, sums, unroll=hb)

        row_receive(index, sent, total_of, consume)
        for k in range(nk):
            total = jnp.sum(sums[k], axis=0, keepdims=True)
            col_s[index, me_s, :, chunk(k)] = total * local_weight[:, k * L : (k + 1) * L]

    weight = local_weight
    v_val = None
    for index in range(1, ROUNDS):
        col_pass(index, row_pass(index, weight))
        v_val = 1.0 / (col_reduce(index, total_of) * cols_all)
        weight = local_weight * v_val

    def barycentric():
        col_out[...] = (EPS * LN2) * (g_first + jnp.log2(v_val))
        pieces = [split(tgt_t[k] * weight[:, k * L : (k + 1) * L]) for k in range(nk)]
        both = jnp.concatenate(
            [
                jnp.concatenate([p[0] for p in pieces], axis=1),
                jnp.concatenate([p[1] for p in pieces], axis=1),
            ],
            axis=0,
        )

        def body(a, carry):
            block = e_b16[pl.ds(a * 4, 4)].reshape(4 * L, cols)
            out = dot_nt(block, both)
            high, low = split(out[:, :width] + out[:, width:])
            start = pl.multiple_of(a * 4 * L, 4 * L)
            bary[pl.ds(start, 4 * L), pl.ds(0, width)] = high
            bary[pl.ds(start, 4 * L), pl.ds(width, width)] = low
            return carry

        lax.fori_loop(0, nb // 4, body, 0, unroll=2)

    sent = row_pass(ROUNDS, weight)
    barycentric()
    inverse = []
    masses = []

    def last_rows(half, mass):
        masses.append(mass)
        recip = 1.0 / mass
        inverse.extend(recip[i : i + 1, :] for i in range(hb))

    row_receive(ROUNDS, sent, total_of, last_rows)
    pieces = [split(src_t[a] * inverse[a]) for a in range(nb)]
    stacked = jnp.concatenate(
        [
            jnp.concatenate([p[0] for p in pieces], axis=1),
            jnp.concatenate([p[1] for p in pieces], axis=1),
        ],
        axis=0,
    )
    out = dot_nn(stacked, bary[...])
    cross[...] = (
        out[:width, :width] + out[:width, width:] + out[width:, :width] + out[width:, width:]
    ).reshape(NPART, width // NPART, width)

    phase = ROW_PHASES + ROUNDS
    for peer in peers_p:
        pltpu.make_async_remote_copy(
            src_ref=cross.at[peer[0] * NX + peer[1] // NZ],
            dst_ref=cross_p.at[me_p],
            send_sem=send_sem.at[phase],
            recv_sem=recv_sem.at[phase],
            device_id=peer,
            device_id_type=MESH,
        ).start()
    cross_p[me_p] = cross[me_p]
    for half in range(HALVES):
        row_out[pl.ds(half * hb, hb), :] = (EPS * LN2) * (
            f_first[half] - math.log2(rows_all) - jnp.log2(masses[half])
        )
    others = cross_p.at[pl.ds(0, len(peers_p))]
    done = pltpu.make_async_remote_copy(
        src_ref=others,
        dst_ref=others,
        send_sem=send_sem.at[phase],
        recv_sem=recv_sem.at[phase],
        device_id=peers_p[0],
        device_id_type=MESH,
    )
    pending.append(done)
    done.wait_recv()
    cross_z[me_z] = jnp.sum(cross_p[...], axis=0)
    send(phase + 1, cross_z, me_z, peers_z).wait_recv()
    cross_g[me_p] = jnp.sum(cross_z[...], axis=0)
    send(phase + 2, cross_g, me_p, peers_p).wait_recv()

    for done in pending:
        done.wait_send()


def polar_kernel(cross_ref, row_ref, col_ref, row_out, col_out, map_out, result, sems):
    stores = [
        pltpu.make_async_copy(row_ref, row_out, sems.at[0]),
        pltpu.make_async_copy(col_ref, col_out, sems.at[1]),
        pltpu.make_async_copy(result, map_out, sems.at[2]),
    ]
    stores[0].start()
    stores[1].start()
    width = result.shape[0]
    matrix = cross_ref[...].reshape(width, width)
    norm = jnp.sum(jnp.sum(matrix * matrix, axis=1, keepdims=True), axis=0, keepdims=True)
    iterate = matrix / jnp.sqrt(norm + 1e-06)

    def newton(_, iterate):
        high, low = split(iterate)
        pair = jnp.concatenate([high, low], axis=1)
        twice = jnp.concatenate(
            [jnp.concatenate([high, high], axis=1), jnp.concatenate([low, low], axis=1)], axis=0
        )
        gram = dot_nt(pair, twice)
        gram = gram[:, :width] + gram[:, width:]
        pair_g = jnp.concatenate(split(gram), axis=1)
        stack = jnp.concatenate([pair, pair], axis=0)
        prod = dot_nn(pair_g, stack)
        return 1.5 * iterate - 0.5 * (prod[:, :width] + prod[:, width:])

    result[...] = lax.fori_loop(0, NEWTON, newton, iterate, unroll=10)
    stores[2].start()
    for store in stores:
        store.wait()


def shards(source, target, start_map, warm_potential):
    rows, width = source.shape
    cols = target.shape[0]
    rows_all, cols_all = rows * lax.axis_size("src"), cols * lax.axis_size("tgt")
    nb, nk = rows // L, cols // L
    phases = ROW_PHASES + ROUNDS + 3
    vmem = pltpu.VMEM
    pots = (jax.ShapeDtypeStruct((nb, L), F32), jax.ShapeDtypeStruct((1, cols), F32))
    part_shape = (NPART, width // NPART, width)
    row_pot, col_pot, cross = pl.pallas_call(
        functools.partial(kernel, rows_all, cols_all),
        out_shape=(*pots, jax.ShapeDtypeStruct(part_shape, F32)),
        in_specs=[pl.BlockSpec(memory_space=pltpu.HBM)] * 4,
        out_specs=[pl.BlockSpec(memory_space=vmem)] * 3,
        scratch_shapes=[
            vmem((rows, width), BF16),
            vmem((cols, width), BF16),
            vmem((width, width), F32),
            vmem((1, cols), F32),
            vmem((rows, width), BF16),
            vmem((nb, L, cols), F32),
            vmem((nb, L, cols), BF16),
            vmem((nb, width, L), F32),
            vmem((nk, width, L), F32),
            vmem((rows, 2 * width), BF16),
            vmem((HALVES, L, L), F32),
            vmem(part_shape, F32),
            vmem((ROUNDS + 1, HALVES, NZ, nb // HALVES, L), F32),
            vmem((ROUNDS + 1, HALVES, NX, nb // HALVES, L), F32),
            vmem((ROUNDS, NSRC, 1, cols), F32),
            vmem(part_shape, F32),
            vmem((NZ, *part_shape[1:]), F32),
            pltpu.SemaphoreType.DMA((phases,)),
            pltpu.SemaphoreType.DMA((phases,)),
            pltpu.SemaphoreType.DMA((4,)),
        ],
        compiler_params=pltpu.CompilerParams(
            collective_id=0, has_side_effects=True, vmem_limit_bytes=40 << 20
        ),
        name="sinkhorn",
    )(
        *(
            pltpu.with_memory_space_constraint(arg, pltpu.HBM)
            for arg in (source, target, start_map, warm_potential.reshape(1, cols))
        )
    )
    row_pot, col_pot, new_map = pl.pallas_call(
        polar_kernel,
        out_shape=(*pots, jax.ShapeDtypeStruct((width, width), F32)),
        in_specs=[pl.BlockSpec(memory_space=vmem)] * 3,
        out_specs=[pl.BlockSpec(memory_space=pltpu.HBM)] * 3,
        scratch_shapes=[vmem((width, width), F32), pltpu.SemaphoreType.DMA((3,))],
        compiler_params=pltpu.CompilerParams(vmem_limit_bytes=8 << 20),
        name="polar",
    )(cross, row_pot, col_pot)
    return row_pot.reshape(rows), col_pot.reshape(cols), new_map


def solution(mesh):
    placed = (P("src", None), P("tgt", None), P(), P("tgt"))
    return jax.shard_map(
        shards,
        mesh=mesh,
        in_specs=placed,
        out_specs=(P("src"), P("tgt"), P()),
        check_vma=False,
    )
```
